512 devices in a mesh: val: 4 (over z_lo), cond: 16 (over y, z_hi), gcol: 8 (over x, core).
Axes of the slice: x: 4, y: 4, z: 16 (z_hi: 4, z_lo: 4; z = z_hi * 4 + z_lo), core: 2. Of those that a mesh axis runs over, the one named last changes fastest.
Arguments:
- psi_val: bfloat16 [2, 16, 72, 5184], P(None, 'val', 'gcol'), may hold values from -6 to 6
- psi_cond: bfloat16 [2, 32, 72, 5184], P(None, 'cond', 'gcol'), may hold values from -6 to 6
- energy_val: float32 [16], P('val'), may hold values from -12 to -2
- energy_cond: float32 [32], P('cond'), may hold values from 0.5 to 8
- occupancy: int32 [16], P('val'), may hold values from 1 to 2
- gmap: int32 [3, 5120], replicated, may hold values from 0 to 71, as said below
Outputs:
- chi: float32 [2, 5120, 5120], P(None, ('val', 'cond'), 'gcol')
The draws below stay inside these ranges and needn't reach their ends.
Inputs may be any that keep to these rules, and one draw needn't show every extreme that they name: `gmap`: the 5120 columns are distinct grid frequencies: the 5120 of smallest kx^2 + ky^2 + kz^2 when each coordinate k is read as k - 72 where it exceeds 72 / 2 (ties at the outermost radius taken in any way), in any order.
All inputs are finite; a program needn't handle non-finite values.
Results may differ from the reference program's by a relative error of at most 0.0039.
Values may be sent and summed in bfloat16 or wider, within the bound.
A program may use at most 128 MiB of HBM per device.

```python
import math
import jax
import jax.numpy as jnp
from jax import lax

NX = 72
NY = 72
NZ = 72
NG = 5120
NV = 16
NC = 32


def folded(coord_value, length):
    return jnp.where(coord_value > length // 2, coord_value - length, coord_value)


def draw_gmap(key, part):
    key = jax.random.fold_in(key, 7)
    cell_count = NX * NY * NZ
    cell_index = jnp.arange(cell_count, dtype=jnp.int32)
    coord_x = cell_index // (NY * NZ)
    coord_y = cell_index // NZ % NY
    coord_z = cell_index % NZ
    radius = folded(coord_x, NX) ** 2 + folded(coord_y, NY) ** 2 + folded(coord_z, NZ) ** 2
    first_key, second_key = jax.random.split(key)
    tie_break = jax.random.permutation(first_key, cell_count).astype(jnp.int32)
    ranking = radius * cell_count + tie_break
    chosen = jnp.argsort(ranking, stable=True)[:NG]
    chosen = chosen[jax.random.permutation(second_key, NG)]
    return jnp.stack([coord_x[chosen], coord_y[chosen], coord_z[chosen]]).astype(jnp.int32)


def set_ends(entries, key, least, high):
    spot = [jax.random.randint(jax.random.fold_in(key, axis), (), 0, length) for axis, length in enumerate(entries.shape)]
    widest = entries.shape.index(max(entries.shape))
    beside = spot[:widest] + [(spot[widest] + 1) % entries.shape[widest]] + spot[widest + 1:]
    return entries.at[tuple(spot)].set(least).at[tuple(beside)].set(high)


def shard_levels(own_key, extent, cuts, least, largest):
    loudness = 1.0
    for axis_at, parts in cuts:
        steps = jax.random.uniform(jax.random.fold_in(jax.random.fold_in(own_key, 6), axis_at), (parts,), jnp.float32, least / len(cuts), largest / len(cuts))
        loudness = loudness * jnp.repeat(jnp.exp(steps), extent[axis_at] // parts).reshape((-1,) + (1,) * (len(extent) - 1 - axis_at))
    return loudness


def noise(own_key, shape, width, most, cuts=(), kind=jnp.bfloat16):
    entries = width * jax.random.normal(own_key, shape, jnp.float32)
    if cuts:
        entries = entries * shard_levels(own_key, shape, cuts, -0.22, 0.18)
    return jnp.clip(entries, -most, most).astype(kind)


def setup_inputs(seed: int = 0) -> dict:
    key_of = jax.random.split(jax.random.key(seed), 7)
    return {
        "psi_val": noise(key_of[0], (2, NV, NZ, NX * NY), 1.0, 6.0, ((1, 4), (2, 8))),
        "psi_cond": noise(key_of[1], (2, NC, NZ, NX * NY), 1.0, 6.0, ((1, 16), (2, 8))),
        "energy_val": jnp.clip(-12.0 + 10.0 * jax.random.uniform(key_of[2], (NV,), jnp.float32) ** shard_levels(key_of[2], (NV,), ((0, 4),), -0.2, 0.2), -12.0, -2.0),
        "energy_cond": jnp.clip(0.5 + 7.5 * jax.random.uniform(key_of[3], (NC,), jnp.float32) ** shard_levels(key_of[3], (NC,), ((0, 16),), -0.2, 0.2), 0.5, 8.0),
        "occupancy": set_ends(jax.random.randint(key_of[4], (NV,), 1, 3), jax.random.fold_in(key_of[4], 1), 1, 2).astype(jnp.int32),
        "gmap": draw_gmap(jax.random.fold_in(key_of[6], 71), 0),
    }


def depth_phases(depth_size, positions, freq_z):
    products = freq_z[:, None] * positions[None, :] % depth_size
    angles = products.astype(jnp.float32) * (2.0 * math.pi / depth_size)
    normal_scale = 1.0 / math.sqrt(depth_size)
    return (jnp.cos(angles) * normal_scale, jnp.sin(angles) * normal_scale)

def reference(psi_val, psi_cond, energy_val, energy_cond, occupancy, gmap):
    grid_rows = gmap[0] * NY + gmap[1]
    cosine_table, sine_table = depth_phases(NZ, jnp.arange(NZ, dtype=jnp.int32), gmap[2])
    conduction = psi_cond.astype(jnp.float32)
    high = lax.Precision.HIGHEST

    def band_elements(valence):
        valence = valence.astype(jnp.float32)
        real_pair = valence[0][None] * conduction[0] + valence[1][None] * conduction[1]
        imag_pair = valence[0][None] * conduction[1] - valence[1][None] * conduction[0]
        complex_field = lax.complex(real_pair, imag_pair).reshape(NC, NZ, NX, NY)
        spectrum = jnp.fft.fft2(complex_field, axes=(2, 3), norm='ortho').reshape(NC, NZ, NX * NY)
        picked = spectrum[:, :, grid_rows]
        real_picked = jnp.real(picked)
        imag_picked = jnp.imag(picked)
        real_part = jnp.einsum('czg,gz->cg', real_picked, cosine_table, precision=high) + jnp.einsum('czg,gz->cg', imag_picked, sine_table, precision=high)
        imag_part = jnp.einsum('czg,gz->cg', imag_picked, cosine_table, precision=high) - jnp.einsum('czg,gz->cg', real_picked, sine_table, precision=high)
        return jnp.stack([real_part, imag_part])
    elements = lax.map(band_elements, jnp.moveaxis(psi_val, 1, 0))
    elements = jnp.moveaxis(elements, 1, 0).reshape(2, NV * NC, NG)
    factor = (occupancy.astype(jnp.float32)[:, None] / (energy_cond[None, :] - energy_val[:, None])).reshape(NV * NC)
    plain_elements = elements.astype(jnp.bfloat16)
    weighted = (elements * factor[None, :, None]).astype(jnp.bfloat16)
    left_side = plain_elements.astype(jnp.float32)
    right_side = weighted.astype(jnp.float32)
    real_part = jnp.dot(left_side[0].T, right_side[0], precision=high) + jnp.dot(left_side[1].T, right_side[1], precision=high)
    imag_part = jnp.dot(left_side[1].T, right_side[0], precision=high) - jnp.dot(left_side[0].T, right_side[1], precision=high)
    pair_scale = 1.0 / math.sqrt(NV * NC)
    return jnp.stack([real_part, imag_part]) * pair_scale
```

```python
import math

import jax
import jax.numpy as jnp
import numpy as np
from jax import lax
from jax.experimental import pallas as pl
from jax.experimental.pallas import tpu as pltpu
from jax.sharding import PartitionSpec as P

MESH = pl.DeviceIdType.MESH
LENGTH = 72
NG = 5120
REACH = 10
SIDE = 2 * REACH + 1
HALF = (REACH + 1) * SIDE
CHUNK_X = 16
CHUNK = CHUNK_X * LENGTH
CHUNKS = 5
DEPTH = 9
WIDTH = 640
ROWS = 80
PLANES = 144
F32 = jnp.float32
BF16 = jnp.bfloat16


def split_bf16(table):
    high = table.astype(np.float32).astype(jnp.bfloat16)
    low = (table - high.astype(np.float64)).astype(np.float32).astype(jnp.bfloat16)
    return high, low


def plane_tables():
    point = np.arange(CHUNK)
    column = np.arange(HALF)
    kx, ky = column // SIDE, column % SIDE - REACH
    turns = (point[:, None] // LENGTH * kx[None] + point[:, None] % LENGTH * ky[None]) % LENGTH
    angles = turns * (2.0 * math.pi / LENGTH)
    table = np.zeros((CHUNK, 512))
    table[:, :HALF] = np.cos(angles) / LENGTH
    table[:, 256 : 256 + HALF] = np.sin(angles) / LENGTH
    high, low = split_bf16(table)
    turned = np.zeros((16, 256), np.float32)
    for chunk in range(CHUNKS):
        shift = (kx * CHUNK_X * chunk) % LENGTH * (2.0 * math.pi / LENGTH)
        turned[2 * chunk, :HALF] = np.cos(shift)
        turned[2 * chunk + 1, :HALF] = np.sin(shift)
    return np.stack([high, low]), turned


def depth_tables():
    kz = np.arange(SIDE) - REACH
    out = np.zeros((8, 64, 256), jnp.bfloat16)
    for group in range(8):
        z = group * DEPTH + np.arange(DEPTH)
        angles = (z[:, None] * kz[None]) % LENGTH * (2.0 * math.pi / LENGTH)
        rows = np.concatenate([np.cos(angles), np.sin(angles)]) / math.sqrt(LENGTH)
        high, low = split_bf16(rows)
        out[group, 0:18, HALF : HALF + SIDE] = high
        out[group, 32:50, HALF : HALF + SIDE] = low
    return out


def dot(a, b):
    return lax.dot_general(a, b, (((1,), (0,)), ((), ())), preferred_element_type=F32)


def kernel(
    val_hbm, cond_hbm, gmap_ref, ev_ref, ec_ref, occ_ref, table_hbm, turn_ref, depth_ref,
    out_ref,
    val_ref, cond_ref, table_ref, index_ref, high_ref, low_ref, left_ref, right_ref,
    part, sib, xout, xin, gathered, row_buf,
    in_sem, sib_s, sib_r, xs, xr, zs, zr, ys, yr, rs, rr,
):
    z_lo = lax.axis_index("val")
    cond = lax.axis_index("cond")
    gcol = lax.axis_index("gcol")
    y, z_hi = cond // 4, cond % 4
    z = z_hi * 4 + z_lo
    x, core = gcol // 2, gcol % 2

    def device(x_at, y_at, z_at, core_at):
        return (z_at % 4, y_at * 4 + z_at // 4, x_at * 2 + core_at)

    def z_peer(step):
        return device(x, y, (z + step + 16) % 16, core)

    def y_peer(step):
        return device(x, (y + step) % 4, z, core)

    def x_peer(step):
        return device((x + step) % 4, y, z, core)

    def g_peer(step):
        return (z_lo, cond, (gcol + step) % 8)

    def remote(src, dst, send, recv, target):
        return pltpu.make_async_remote_copy(
            src_ref=src, dst_ref=dst, send_sem=send, recv_sem=recv, device_id=target, device_id_type=MESH
        )

    peers = [g_peer(s) for s in range(1, 8)]
    peers += [z_peer(s) for s in (1, 2, 4, 8, 12, 14, 15)]
    peers += [y_peer(s) for s in (1, 2, 3)]
    barrier = pltpu.get_barrier_semaphore()
    for peer in peers:
        pl.semaphore_signal(barrier, inc=1, device_id=peer, device_id_type=MESH)

    loads = [
        pltpu.make_async_copy(val_hbm, val_ref, in_sem.at[0]),
        pltpu.make_async_copy(cond_hbm, cond_ref, in_sem.at[1]),
        pltpu.make_async_copy(table_hbm, table_ref, in_sem.at[2]),
    ]
    for load in loads:
        load.start()

    freq = gmap_ref[...]
    freq = jnp.where(freq > LENGTH // 2, freq - LENGTH, freq)
    kx, ky, kz = freq[0:1], freq[1:2], freq[2:3]
    flip = kx < 0
    index_ref[0:1, :] = jnp.where(flip, -kx, kx) * SIDE + jnp.where(flip, -ky, ky) + REACH
    index_ref[1:2, :] = jnp.where(flip, -1, 1)
    index_ref[2:3, :] = kz + (REACH + HALF)
    pad = (CHUNKS - 1) * PLANES
    high_ref[pad:, 576:] = jnp.zeros((PLANES, CHUNK - 576), BF16)
    low_ref[pad:, 576:] = jnp.zeros((PLANES, CHUNK - 576), BF16)
    loads[0].wait()
    loads[1].wait()

    for chunk in range(CHUNKS):
        for begin, width in ((0, 384), (384, 384), (768, 384)) if chunk < 4 else ((0, 384), (384, 192)):
            span = pl.ds(chunk * CHUNK + begin, width)
            v = [[val_ref[c, b, :, span].astype(F32) for b in range(4)] for c in range(2)]
            w = [[cond_ref[c, b, :, span].astype(F32) for b in range(2)] for c in range(2)]
            sub = lax.broadcasted_iota(jnp.int32, (8, width), 0)

            def last(rows, count):
                spread = [jnp.broadcast_to(r[8:9], (8, width)) for r in rows]
                if count == 2:
                    return jnp.where(sub % 2 == 0, spread[0], spread[1])
                lower = jnp.where(sub < 2, spread[0], spread[1])
                upper = jnp.where(sub < 6, spread[2], spread[3])
                return jnp.where(sub < 4, lower, upper)

            real, imag = [], []
            for b in range(4):
                for d in range(2):
                    vr, vi, wr, wi = v[0][b][0:8], v[1][b][0:8], w[0][d][0:8], w[1][d][0:8]
                    real.append(vr * wr + vi * wi)
                    imag.append(vr * wi - vi * wr)
            vr, vi, wr, wi = last(v[0], 4), last(v[1], 4), last(w[0], 2), last(w[1], 2)
            real.append(vr * wr + vi * wi)
            imag.append(vr * wi - vi * wr)
            field = jnp.concatenate(real + imag, axis=0)
            high = field.astype(BF16)
            low = (field - high.astype(F32)).astype(BF16)
            rows = slice(chunk * PLANES, (chunk + 1) * PLANES)
            high_ref[rows, begin : begin + width] = high
            low_ref[rows, begin : begin + width] = low

    loads[2].wait()
    planes = dot(high_ref[...], table_ref[0]) + dot(low_ref[...], table_ref[0]) + dot(high_ref[...], table_ref[1])
    cos_sum = planes[0:PLANES, 0:256]
    sin_sum = planes[0:PLANES, 256:512]
    for chunk in range(1, CHUNKS):
        at = chunk * PLANES
        c_part, s_part = planes[at : at + PLANES, 0:256], planes[at : at + PLANES, 256:512]
        c_turn, s_turn = turn_ref[2 * chunk : 2 * chunk + 1, :], turn_ref[2 * chunk + 1 : 2 * chunk + 2, :]
        cos_sum += c_turn * c_part - s_turn * s_part
        sin_sum += s_turn * c_part + c_turn * s_part

    def by_plane(rows):
        first = jnp.swapaxes(rows[0:64].reshape(8, 8, 256), 0, 1).reshape(64, 256)
        return jnp.concatenate([first, rows[64:72]], axis=0)

    even = jnp.concatenate([by_plane(cos_sum[0:72]), by_plane(cos_sum[72:144])], axis=0)
    odd = jnp.concatenate([by_plane(sin_sum[72:144]), -by_plane(sin_sum[0:72])], axis=0)
    even_high, odd_high = even.astype(BF16), odd.astype(BF16)
    left_ref[0:144, :] = even_high
    left_ref[144:288, :] = (even - even_high.astype(F32)).astype(BF16)
    left_ref[288:352, :] = depth_ref[gcol]
    right_ref[0:144, :] = odd_high
    right_ref[144:288, :] = (odd - odd_high.astype(F32)).astype(BF16)

    place = lax.broadcasted_iota(jnp.int32, (256, 256), 0)

    def block(step):
        target = (x + 3 - step) % 4
        for piece in range(5):
            span = pl.ds(pl.multiple_of(target * 1280 + piece * 256, 256), 256)
            hit = place == index_ref[0:1, span]
            phase = place == index_ref[2:3, span]
            pick = jnp.where(hit | phase, 1.0, 0.0).astype(BF16)
            signed = jnp.where(hit, index_ref[1:2, span].astype(F32), 0.0).astype(BF16)
            first = dot(left_ref[...], pick)
            second = dot(right_ref[...], signed)
            values = first[0:144] + first[144:288] + second[0:144] + second[144:288]
            phases = first[288:306] + first[320:338]
            real, imag = None, None
            for d in range(DEPTH):
                re, im = values[8 * d : 8 * d + 8], values[72 + 8 * d : 80 + 8 * d]
                c, s = phases[d : d + 1], phases[DEPTH + d : DEPTH + d + 1]
                r_term, i_term = re * c + im * s, im * c - re * s
                real = r_term if real is None else real + r_term
                imag = i_term if imag is None else imag + i_term
            both = jnp.concatenate([real, imag], axis=0)
            for q in range(2):
                at = piece * 256 + q * 128
                part[step, at // WIDTH, :, at % WIDTH : at % WIDTH + 128] = both[:, q * 128 : (q + 1) * 128]

    sib_copies = [
        remote(part.at[j, 1 - core], sib.at[j], sib_s.at[j], sib_r.at[j], device(x, y, z, 1 - core)) for j in range(4)
    ]
    x_copies = [remote(xout.at[j], xin.at[j], xs.at[j], xr.at[j], x_peer(3 - j)) for j in range(3)]
    for j in range(4):
        block(j)
        if j == 0:
            pl.semaphore_wait(barrier, len(peers))
        sib_copies[j].start()
        if j > 0:
            sib_copies[j - 1].wait_recv()
            xout[j - 1] = part[j - 1, core] + sib[j - 1]
            x_copies[j - 1].start()

    pair = lax.broadcasted_iota(jnp.int32, (16, 1), 0) % 8
    e_val = jnp.zeros((16, 1), F32)
    e_cond = jnp.zeros((16, 1), F32)
    occupied = jnp.zeros((16, 1), F32)
    for b in range(4):
        e_val = jnp.where(pair // 2 == b, ev_ref[b], e_val)
        occupied = jnp.where(pair // 2 == b, occ_ref[b].astype(F32), occupied)
    for d in range(2):
        e_cond = jnp.where(pair % 2 == d, ec_ref[d], e_cond)
    factor = jnp.sqrt(occupied / (e_cond - e_val) * (1.0 / math.sqrt(512.0)))

    sib_copies[3].wait_recv()
    total = part[3, core] + sib[3]
    for j in range(3):
        x_copies[j].wait_recv()
        total += xin[j]
    gathered[0, 0] = (total * factor).astype(BF16)

    z_copies = [
        remote(gathered.at[0, 0], gathered.at[0, a], zs.at[a], zr.at[a], z_peer(4 * a)) for a in (2, 1, 3)
    ]
    for copy in z_copies:
        copy.start()
    for copy in z_copies:
        copy.wait_recv()
    near = [(1, 0, 4, 4), (15, 0, 12, 4), (2, 1, 8, 2), (14, 0, 10, 2)]
    near_copies = [
        remote(gathered.at[0, pl.ds(src, n)], gathered.at[0, pl.ds(dst, n)], zs.at[4 + i], zr.at[4 + i], z_peer(step))
        for i, (step, src, dst, n) in enumerate(near)
    ]
    for copy in near_copies:
        copy.start()
    for copy in near_copies:
        copy.wait_recv()
    y_copies = {j: remote(gathered.at[0], gathered.at[j], ys.at[j], yr.at[j], y_peer(j)) for j in (1, 3, 2)}
    for j in (1, 3, 2):
        y_copies[j].start()

    is_source = gcol == z_lo * 2 + cond // 8
    offset = cond % 8 * ROWS
    chosen = jnp.where(
        lax.broadcasted_iota(jnp.int32, (ROWS, WIDTH), 1)
        == lax.broadcasted_iota(jnp.int32, (ROWS, WIDTH), 0) + offset,
        1.0,
        0.0,
    ).astype(BF16)
    k_row = lax.broadcasted_iota(jnp.int32, (256, 256), 0)
    k_col = lax.broadcasted_iota(jnp.int32, (256, 256), 1)
    is_real = k_col // 8 % 2 == 0
    turn_i = jnp.where(
        is_real & (k_row == k_col + 8), 1.0, jnp.where(~is_real & (k_row == k_col - 8), -1.0, 0.0)
    ).astype(BF16)

    def row_copy(j, step):
        return remote(row_buf.at[j], row_buf.at[j], rs.at[j, step], rr.at[j], g_peer(step))

    def share_rows(j):
        @pl.when(is_source)
        def _():
            columns = gathered[j].reshape(256, WIDTH)
            rows = lax.dot_general(chosen, columns, (((1,), (1,)), ((), ())), preferred_element_type=F32)
            row_buf[j] = rows.astype(BF16)
            for step in range(1, 8):
                row_copy(j, step).start()

    def use(j, first):
        @pl.when(jnp.logical_not(is_source))
        def _():
            row_copy(j, 1).wait_recv()

        rows = row_buf[j]
        rows_i = dot(rows, turn_i).astype(BF16)
        columns = gathered[j].reshape(256, WIDTH)
        real, imag = dot(rows, columns), dot(rows_i, columns)
        if first:
            out_ref[0] = real
            out_ref[1] = imag
        else:
            out_ref[0] += real
            out_ref[1] += imag

    share_rows(0)
    y_copies[1].wait_recv()
    share_rows(1)
    use(0, True)
    y_copies[3].wait_recv()
    share_rows(3)
    use(1, False)
    y_copies[2].wait_recv()
    share_rows(2)
    use(3, False)
    use(2, False)

    @pl.when(is_source)
    def _():
        for j in range(4):
            for step in range(1, 8):
                row_copy(j, step).wait_send()

    for copy in sib_copies + x_copies + z_copies + near_copies + list(y_copies.values()):
        copy.wait_send()


def shards(psi_val, psi_cond, energy_val, energy_cond, occupancy, gmap):
    table, turned = plane_tables()
    vmem = pl.BlockSpec(memory_space=pltpu.VMEM)
    smem = pl.BlockSpec(memory_space=pltpu.SMEM)
    anywhere = pl.BlockSpec(memory_space=pl.ANY)
    dma = pltpu.SemaphoreType.DMA
    return pl.pallas_call(
        kernel,
        out_shape=jax.ShapeDtypeStruct((2, ROWS, WIDTH), F32),
        in_specs=[anywhere, anywhere, vmem, smem, smem, smem, anywhere, vmem, vmem],
        out_specs=vmem,
        scratch_shapes=[
            pltpu.VMEM((2, 4, DEPTH, 5184), BF16),
            pltpu.VMEM((2, 2, DEPTH, 5184), BF16),
            pltpu.VMEM((2, CHUNK, 512), BF16),
            pltpu.VMEM((8, NG), jnp.int32),
            pltpu.VMEM((CHUNKS * PLANES, CHUNK), BF16),
            pltpu.VMEM((CHUNKS * PLANES, CHUNK), BF16),
            pltpu.VMEM((352, 256), BF16),
            pltpu.VMEM((288, 256), BF16),
            pltpu.VMEM((4, 2, 16, WIDTH), F32),
            pltpu.VMEM((4, 16, WIDTH), F32),
            pltpu.VMEM((3, 16, WIDTH), F32),
            pltpu.VMEM((3, 16, WIDTH), F32),
            pltpu.VMEM((4, 16, 16, WIDTH), BF16),
            pltpu.VMEM((4, ROWS, 256), BF16),
            dma((3,)), dma((4,)), dma((4,)), dma((3,)), dma((3,)),
            dma((8,)), dma((8,)), dma((4,)), dma((4,)), dma((4, 8)), dma((4,)),
        ],
        compiler_params=pltpu.CompilerParams(
            collective_id=0, has_side_effects=True, vmem_limit_bytes=48 * 1024 * 1024
        ),
        cost_estimate=pl.CostEstimate(flops=8_000_000_000, bytes_accessed=6_000_000, transcendentals=0),
    )(
        psi_val, psi_cond, gmap, energy_val, energy_cond, occupancy,
        jnp.asarray(table), jnp.asarray(turned), jnp.asarray(depth_tables()),
    )


def solution(mesh):
    return jax.shard_map(
        shards,
        mesh=mesh,
        in_specs=(
            P(None, "val", "gcol", None),
            P(None, "cond", "gcol", None),
            P("val"),
            P("cond"),
            P("val"),
            P(),
        ),
        out_specs=P(None, ("val", "cond"), "gcol"),
        check_vma=False,
    )
```

```python
import math

import jax
import jax.numpy as jnp
import numpy as np
from jax import lax
from jax.experimental import pallas as pl
from jax.experimental.pallas import tpu as pltpu
from jax.sharding import PartitionSpec as P

MESH = pl.DeviceIdType.MESH
LENGTH = 72
NG = 5120
REACH = 10
SIDE = 2 * REACH + 1
HALF = (REACH + 1) * SIDE
CHUNK_X = 16
CHUNK = CHUNK_X * LENGTH
CHUNKS = 5
DEPTH = 9
WIDTH = 640
ROWS = 80
PLANES = 144
F32 = jnp.float32
BF16 = jnp.bfloat16


def split_bf16(table):
    high = table.astype(np.float32).astype(jnp.bfloat16)
    low = (table - high.astype(np.float64)).astype(np.float32).astype(jnp.bfloat16)
    return high, low


def plane_tables():
    point = np.arange(CHUNK)
    column = np.arange(HALF)
    kx, ky = column // SIDE, column % SIDE - REACH
    turns = (point[:, None] // LENGTH * kx[None] + point[:, None] % LENGTH * ky[None]) % LENGTH
    angles = turns * (2.0 * math.pi / LENGTH)
    table = np.zeros((CHUNK, 512))
    table[:, :HALF] = np.cos(angles) / LENGTH
    table[:, 256 : 256 + HALF] = np.sin(angles) / LENGTH
    high, low = split_bf16(table)
    turned = np.zeros((16, 256), np.float32)
    for chunk in range(CHUNKS):
        shift = (kx * CHUNK_X * chunk) % LENGTH * (2.0 * math.pi / LENGTH)
        turned[2 * chunk, :HALF] = np.cos(shift)
        turned[2 * chunk + 1, :HALF] = np.sin(shift)
    return np.stack([high, low]), turned


def depth_tables():
    kz = np.arange(SIDE) - REACH
    out = np.zeros((8, 64, 256), jnp.bfloat16)
    for group in range(8):
        z = group * DEPTH + np.arange(DEPTH)
        angles = (z[:, None] * kz[None]) % LENGTH * (2.0 * math.pi / LENGTH)
        rows = np.concatenate([np.cos(angles), np.sin(angles)]) / math.sqrt(LENGTH)
        high, low = split_bf16(rows)
        out[group, 0:18, HALF : HALF + SIDE] = high
        out[group, 32:50, HALF : HALF + SIDE] = low
    return out


def dot(a, b):
    return lax.dot_general(a, b, (((1,), (0,)), ((), ())), preferred_element_type=F32)


def kernel(
    val_hbm, cond_hbm, gmap_hbm, ev_hbm, ec_hbm, occ_hbm, table_hbm, turn_hbm, depth_hbm,
    out_ref,
    val_ref, cond_ref, gmap_ref, ev_ref, ec_ref, occ_ref, table_ref, turn_ref, depth_ref, index_ref, high_ref, low_ref, left_ref, right_ref,
    part, sib, xout, xin, gathered, row_buf,
    in_sem, sib_s, sib_r, xs, xr, fs, fr, zs, zr, ys, yr, rs, rr,
):
    z_lo = lax.axis_index("val")
    cond = lax.axis_index("cond")
    gcol = lax.axis_index("gcol")
    y, z_hi = cond // 4, cond % 4
    z = z_hi * 4 + z_lo
    x, core = gcol // 2, gcol % 2

    def device(x_at, y_at, z_at, core_at):
        return (z_at % 4, y_at * 4 + z_at // 4, x_at * 2 + core_at)

    def z_peer(step):
        return device(x, y, (z + step + 16) % 16, core)

    def y_peer(step):
        return device(x, (y + step) % 4, z, core)

    def x_peer(step):
        return device((x + step) % 4, y, z, core)

    def g_peer(step):
        return (z_lo, cond, (gcol + step) % 8)

    def remote(src, dst, send, recv, target):
        return pltpu.make_async_remote_copy(
            src_ref=src, dst_ref=dst, send_sem=send, recv_sem=recv, device_id=target, device_id_type=MESH
        )

    peers = [g_peer(s) for s in range(1, 8)]
    peers += [z_peer(s) for s in (1, 2, 4, 8, 12, 14, 15)]
    peers += [y_peer(s) for s in (1, 2, 3)]
    barrier = pltpu.get_barrier_semaphore()
    for peer in peers:
        pl.semaphore_signal(barrier, inc=1, device_id=peer, device_id_type=MESH)

    loads = [
        pltpu.make_async_copy(src, dst, in_sem.at[n])
        for n, (src, dst) in enumerate(
            [
                (gmap_hbm, gmap_ref), (val_hbm, val_ref), (cond_hbm, cond_ref), (table_hbm, table_ref),
                (turn_hbm, turn_ref), (depth_hbm.at[gcol], depth_ref),
                (ev_hbm, ev_ref), (ec_hbm, ec_ref), (occ_hbm, occ_ref),
            ]
        )
    ]
    for load in loads:
        load.start()
    loads[0].wait()

    freq = gmap_ref[...]
    freq = jnp.where(freq > LENGTH // 2, freq - LENGTH, freq)
    kx, ky, kz = freq[0:1], freq[1:2], freq[2:3]
    flip = kx < 0
    index_ref[0:1, :] = jnp.where(flip, -kx, kx) * SIDE + jnp.where(flip, -ky, ky) + REACH
    index_ref[1:2, :] = jnp.where(flip, -1, 1)
    index_ref[2:3, :] = kz + (REACH + HALF)
    pad = (CHUNKS - 1) * PLANES
    high_ref[pad:, 576:] = jnp.zeros((PLANES, CHUNK - 576), BF16)
    low_ref[pad:, 576:] = jnp.zeros((PLANES, CHUNK - 576), BF16)
    loads[1].wait()
    loads[2].wait()

    for chunk in range(CHUNKS):
        for begin, width in ((0, 384), (384, 384), (768, 384)) if chunk < 4 else ((0, 384), (384, 192)):
            span = pl.ds(chunk * CHUNK + begin, width)
            sub = lax.broadcasted_iota(jnp.int32, (8, width), 0)
            real, imag = [], []
            for d in range(DEPTH):
                v, w = [], []
                for c in range(2):
                    four = val_ref[c, d, :, span].astype(F32)
                    v.append(jnp.concatenate([four, four], axis=0))
                    two = cond_ref[c, d, :, span].astype(F32)
                    spread = [jnp.broadcast_to(two[i : i + 1], (8, width)) for i in range(2)]
                    w.append(jnp.where(sub < 4, spread[0], spread[1]))
                real.append(v[0] * w[0] + v[1] * w[1])
                imag.append(v[0] * w[1] - v[1] * w[0])
            field = jnp.concatenate(real + imag, axis=0)
            high = field.astype(BF16)
            low = (field - high.astype(F32)).astype(BF16)
            rows = slice(chunk * PLANES, (chunk + 1) * PLANES)
            high_ref[rows, begin : begin + width] = high
            low_ref[rows, begin : begin + width] = low

    for load in loads[3:]:
        load.wait()
    planes = dot(high_ref[...], table_ref[0]) + dot(low_ref[...], table_ref[0]) + dot(high_ref[...], table_ref[1])
    cos_sum = planes[0:PLANES, 0:256]
    sin_sum = planes[0:PLANES, 256:512]
    for chunk in range(1, CHUNKS):
        at = chunk * PLANES
        c_part, s_part = planes[at : at + PLANES, 0:256], planes[at : at + PLANES, 256:512]
        c_turn, s_turn = turn_ref[2 * chunk : 2 * chunk + 1, :], turn_ref[2 * chunk + 1 : 2 * chunk + 2, :]
        cos_sum += c_turn * c_part - s_turn * s_part
        sin_sum += s_turn * c_part + c_turn * s_part

    even = cos_sum
    odd = jnp.concatenate([sin_sum[72:144], -sin_sum[0:72]], axis=0)
    even_high, odd_high = even.astype(BF16), odd.astype(BF16)
    left_ref[0:144, :] = even_high
    left_ref[144:288, :] = (even - even_high.astype(F32)).astype(BF16)
    left_ref[288:352, :] = depth_ref[...]
    right_ref[0:144, :] = odd_high
    right_ref[144:288, :] = (odd - odd_high.astype(F32)).astype(BF16)

    place = lax.broadcasted_iota(jnp.int32, (256, 256), 0)

    def block(step):
        target = (x + 3 - step) % 4
        for piece in range(5):
            span = pl.ds(pl.multiple_of(target * 1280 + piece * 256, 256), 256)
            hit = place == index_ref[0:1, span]
            phase = place == index_ref[2:3, span]
            pick = jnp.where(hit | phase, 1.0, 0.0).astype(BF16)
            signed = jnp.where(hit, index_ref[1:2, span].astype(F32), 0.0).astype(BF16)
            first = dot(left_ref[...], pick)
            second = dot(right_ref[...], signed)
            values = first[0:144] + first[144:288] + second[0:144] + second[144:288]
            phases = first[288:306] + first[320:338]
            real, imag = None, None
            for d in range(DEPTH):
                re, im = values[8 * d : 8 * d + 8], values[72 + 8 * d : 80 + 8 * d]
                c, s = phases[d : d + 1], phases[DEPTH + d : DEPTH + d + 1]
                r_term, i_term = re * c + im * s, im * c - re * s
                real = r_term if real is None else real + r_term
                imag = i_term if imag is None else imag + i_term
            both = jnp.concatenate([real, imag], axis=0)
            for q in range(2):
                at = piece * 256 + q * 128
                part[step, at // WIDTH, :, at % WIDTH : at % WIDTH + 128] = both[:, q * 128 : (q + 1) * 128]

    sib_copies = [
        remote(part.at[j, 1 - core], sib.at[j], sib_s.at[j], sib_r.at[j], device(x, y, z, 1 - core)) for j in range(4)
    ]
    x_copies = [remote(xout.at[j], xin.at[j], xs.at[j], xr.at[j], x_peer(3 - j)) for j in range(3)]
    for j in range(4):
        block(j)
        if j == 0:
            pl.semaphore_wait(barrier, len(peers))
        sib_copies[j].start()
        if j > 0:
            sib_copies[j - 1].wait_recv()
            xout[j - 1] = part[j - 1, core] + sib[j - 1]
            x_copies[j - 1].start()

    pair = lax.broadcasted_iota(jnp.int32, (16, 1), 0) % 8
    e_val = jnp.zeros((16, 1), F32)
    e_cond = jnp.zeros((16, 1), F32)
    occupied = jnp.zeros((16, 1), F32)
    for b in range(4):
        e_val = jnp.where(pair % 4 == b, ev_ref[b], e_val)
        occupied = jnp.where(pair % 4 == b, occ_ref[b].astype(F32), occupied)
    for d in range(2):
        e_cond = jnp.where(pair // 4 == d, ec_ref[d], e_cond)
    factor = jnp.sqrt(occupied / (e_cond - e_val) * (1.0 / math.sqrt(512.0)))

    sib_copies[3].wait_recv()
    total = part[3, core] + sib[3]
    for j in range(3):
        x_copies[j].wait_recv()
        total += xin[j]
    gathered[z_hi, 0, 0] = (total * factor).astype(BF16)

    far_copies = [
        remote(gathered.at[z_hi, 0, 0], gathered.at[z_hi, 0, 0], fs.at[a], fr.at[z_hi], z_peer(4 * a)) for a in (2, 1, 3)
    ]

    def near_copies(q):
        steps = ((1, 1), (15, 3), (2 - 4 * ((q + 1) // 2 % 2), 2))
        return [
            remote(gathered.at[q, 0, 0], gathered.at[q, 0, m], zs.at[q, m], zr.at[q, m], z_peer(step))
            for step, m in steps
        ]

    def y_copies(q):
        return [remote(gathered.at[q, 0], gathered.at[q, j], ys.at[q, j], yr.at[q, j], y_peer(j)) for j in (1, 3, 2)]

    def pass_on(q):
        @pl.when(z_hi != q)
        def _():
            remote(gathered.at[q, 0, 0], gathered.at[q, 0, 0], fs.at[0], fr.at[q], z_peer(4)).wait_recv()
            for copy in near_copies(q):
                copy.start()

    def share_y(q):
        for copy in near_copies(q):
            copy.wait_recv()
        for copy in y_copies(q):
            copy.start()

    for copy in far_copies:
        copy.start()
    for copy in near_copies(z_hi):
        copy.start()

    is_source = gcol == z_lo * 2 + cond // 8
    offset = cond % 8 * ROWS
    chosen = jnp.where(
        lax.broadcasted_iota(jnp.int32, (ROWS, WIDTH), 1)
        == lax.broadcasted_iota(jnp.int32, (ROWS, WIDTH), 0) + offset,
        1.0,
        0.0,
    ).astype(BF16)
    k_row = lax.broadcasted_iota(jnp.int32, (256, 256), 0)
    k_col = lax.broadcasted_iota(jnp.int32, (256, 256), 1)
    is_real = k_col // 8 % 2 == 0
    turn_i = jnp.where(
        is_real & (k_row == k_col + 8), 1.0, jnp.where(~is_real & (k_row == k_col - 8), -1.0, 0.0)
    ).astype(BF16)

    def row_copy(j, step):
        return remote(row_buf.at[j], row_buf.at[j], rs.at[j, step], rr.at[j], g_peer(step))

    def share_rows(j):
        for copy in y_copies(j):
            copy.wait_recv()

        @pl.when(is_source)
        def _():
            columns = gathered[j].reshape(256, WIDTH)
            rows = lax.dot_general(chosen, columns, (((1,), (1,)), ((), ())), preferred_element_type=F32)
            row_buf[j] = rows.astype(BF16)
            for step in range(1, 8):
                row_copy(j, step).start()

    def use(j, first):
        @pl.when(jnp.logical_not(is_source))
        def _():
            row_copy(j, 1).wait_recv()

        rows = row_buf[j]
        rows_i = dot(rows, turn_i).astype(BF16)
        columns = gathered[j].reshape(256, WIDTH)
        real, imag = dot(rows, columns), dot(rows_i, columns)
        if first:
            out_ref[0] = real
            out_ref[1] = imag
        else:
            out_ref[0] += real
            out_ref[1] += imag

    pass_on(0)
    pass_on(1)
    share_y(0)
    pass_on(3)
    share_y(1)
    share_rows(0)
    pass_on(2)
    share_y(3)
    share_rows(1)
    use(0, True)
    share_y(2)
    share_rows(3)
    use(1, False)
    share_rows(2)
    use(3, False)
    use(2, False)

    @pl.when(is_source)
    def _():
        for j in range(4):
            for step in range(1, 8):
                row_copy(j, step).wait_send()

    for copy in sib_copies + x_copies + far_copies:
        copy.wait_send()
    for q in range(4):
        for copy in near_copies(q) + y_copies(q):
            copy.wait_send()


def shards(psi_val, psi_cond, energy_val, energy_cond, occupancy, gmap):
    table, turned = plane_tables()
    vmem = pl.BlockSpec(memory_space=pltpu.VMEM)
    hbm = pl.BlockSpec(memory_space=pltpu.HBM)
    dma = pltpu.SemaphoreType.DMA
    return pl.pallas_call(
        kernel,
        out_shape=jax.ShapeDtypeStruct((2, ROWS, WIDTH), F32),
        in_specs=[hbm] * 9,
        out_specs=vmem,
        scratch_shapes=[
            pltpu.VMEM((2, DEPTH, 4, 5184), BF16),
            pltpu.VMEM((2, DEPTH, 2, 5184), BF16),
            pltpu.VMEM((3, NG), jnp.int32),
            pltpu.SMEM((4,), F32),
            pltpu.SMEM((2,), F32),
            pltpu.SMEM((4,), jnp.int32),
            pltpu.VMEM((2, CHUNK, 512), BF16),
            pltpu.VMEM((16, 256), F32),
            pltpu.VMEM((64, 256), BF16),
            pltpu.VMEM((8, NG), jnp.int32),
            pltpu.VMEM((CHUNKS * PLANES, CHUNK), BF16),
            pltpu.VMEM((CHUNKS * PLANES, CHUNK), BF16),
            pltpu.VMEM((352, 256), BF16),
            pltpu.VMEM((288, 256), BF16),
            pltpu.VMEM((4, 2, 16, WIDTH), F32),
            pltpu.VMEM((4, 16, WIDTH), F32),
            pltpu.VMEM((3, 16, WIDTH), F32),
            pltpu.VMEM((3, 16, WIDTH), F32),
            pltpu.VMEM((4, 4, 4, 16, WIDTH), BF16),
            pltpu.VMEM((4, ROWS, 256), BF16),
            dma((9,)), dma((4,)), dma((4,)), dma((3,)), dma((3,)),
            dma((4,)), dma((4,)), dma((4, 4)), dma((4, 4)), dma((4, 4)), dma((4, 4)), dma((4, 8)), dma((4,)),
        ],
        compiler_params=pltpu.CompilerParams(
            collective_id=0, has_side_effects=True, vmem_limit_bytes=64 * 1024 * 1024
        ),
        cost_estimate=pl.CostEstimate(flops=8_000_000_000, bytes_accessed=6_000_000, transcendentals=0),
    )(
        jnp.swapaxes(psi_val, 1, 2), jnp.swapaxes(psi_cond, 1, 2), gmap, energy_val, energy_cond, occupancy,
        jnp.asarray(table), jnp.asarray(turned), jnp.asarray(depth_tables()),
    )


def solution(mesh):
    return jax.shard_map(
        shards,
        mesh=mesh,
        in_specs=(
            P(None, "val", "gcol", None),
            P(None, "cond", "gcol", None),
            P("val"),
            P("cond"),
            P("val"),
            P(),
        ),
        out_specs=P(None, ("val", "cond"), "gcol"),
        check_vma=False,
    )
```

```python
import math

import jax
import jax.numpy as jnp
import numpy as np
from jax import lax
from jax.experimental import pallas as pl
from jax.experimental.pallas import tpu as pltpu
from jax.sharding import PartitionSpec as P

MESH = pl.DeviceIdType.MESH
LENGTH = 72
NG = 5120
REACH = 10
SIDE = 2 * REACH + 1
HALF = (REACH + 1) * SIDE
CHUNK_X = 16
CHUNK = CHUNK_X * LENGTH
CHUNKS = 5
DEPTH = 9
WIDTH = 640
ROWS = 80
MAIN = 384
PLANES = 144
F32 = jnp.float32
BF16 = jnp.bfloat16


def split_bf16(table):
    high = table.astype(np.float32).astype(jnp.bfloat16)
    low = (table - high.astype(np.float64)).astype(np.float32).astype(jnp.bfloat16)
    return high, low


def plane_tables():
    point = np.arange(CHUNK)
    column = np.arange(HALF)
    kx, ky = column // SIDE, column % SIDE - REACH
    turns = (point[:, None] // LENGTH * kx[None] + point[:, None] % LENGTH * ky[None]) % LENGTH
    angles = turns * (2.0 * math.pi / LENGTH)
    table = np.zeros((CHUNK, 512))
    table[:, :HALF] = np.cos(angles) / LENGTH
    table[:, 256 : 256 + HALF] = np.sin(angles) / LENGTH
    high, low = split_bf16(table)
    turned = np.zeros((16, 256), np.float32)
    for chunk in range(CHUNKS):
        shift = (kx * CHUNK_X * chunk) % LENGTH * (2.0 * math.pi / LENGTH)
        turned[2 * chunk, :HALF] = np.cos(shift)
        turned[2 * chunk + 1, :HALF] = np.sin(shift)
    return np.stack([high, low]), turned


def depth_tables():
    kz = np.arange(SIDE) - REACH
    out = np.zeros((8, 64, 256), jnp.bfloat16)
    for group in range(8):
        z = group * DEPTH + np.arange(DEPTH)
        angles = (z[:, None] * kz[None]) % LENGTH * (2.0 * math.pi / LENGTH)
        rows = np.concatenate([np.cos(angles), np.sin(angles)]) / math.sqrt(LENGTH)
        high, low = split_bf16(rows)
        out[group, 0:18, HALF : HALF + SIDE] = high
        out[group, 32:50, HALF : HALF + SIDE] = low
    return out


def dot(a, b):
    return lax.dot_general(a, b, (((1,), (0,)), ((), ())), preferred_element_type=F32)


def kernel(
    val_hbm, cond_hbm, gmap_hbm, ev_hbm, ec_hbm, occ_hbm, table_hbm, turn_hbm, depth_hbm,
    out_ref,
    val_ref, cond_ref, gmap_ref, ev_ref, ec_ref, occ_ref, table_ref, turn_ref, depth_ref, index_ref, high_ref, low_ref, left_ref, right_ref,
    part, sib, xout, xin, gathered, row_buf, row_out, row_in,
    in_sem, sib_s, sib_r, xs, xr, fs, fr, zs, zr, ys, yr, rs, rr, ps, pr, vs, vr, us, ur,
):
    z_lo = lax.axis_index("val")
    cond = lax.axis_index("cond")
    gcol = lax.axis_index("gcol")
    y, z_hi = cond // 4, cond % 4
    z = z_hi * 4 + z_lo
    x, core = gcol // 2, gcol % 2

    def device(x_at, y_at, z_at, core_at):
        return (z_at % 4, y_at * 4 + z_at // 4, x_at * 2 + core_at)

    def z_peer(step):
        return device(x, y, (z + step + 16) % 16, core)

    def y_peer(step):
        return device(x, (y + step) % 4, z, core)

    def x_peer(step):
        return device((x + step) % 4, y, z, core)

    def g_peer(step):
        return (z_lo, cond, (gcol + step) % 8)

    def remote(src, dst, send, recv, target):
        return pltpu.make_async_remote_copy(
            src_ref=src, dst_ref=dst, send_sem=send, recv_sem=recv, device_id=target, device_id_type=MESH
        )

    peers = [g_peer(s) for s in range(1, 8)]
    peers += [z_peer(s) for s in (1, 2, 4, 8, 12, 14, 15)]
    peers += [y_peer(s) for s in (1, 2, 3)]
    barrier = pltpu.get_barrier_semaphore()
    for peer in peers:
        pl.semaphore_signal(barrier, inc=1, device_id=peer, device_id_type=MESH)
    is_source = gcol == z_lo * 2 + cond // 8

    @pl.when(is_source)
    def _():
        @pl.loop(0, 64)
        def _(n):
            @pl.when(n != y * 16 + z)
            def _():
                pl.semaphore_signal(
                    barrier, inc=1, device_id=device(x, n // 16, n % 16, core), device_id_type=MESH
                )


    loads = [
        pltpu.make_async_copy(src, dst, in_sem.at[n])
        for n, (src, dst) in enumerate(
            [
                (gmap_hbm, gmap_ref), (val_hbm, val_ref), (cond_hbm, cond_ref), (table_hbm, table_ref),
                (turn_hbm, turn_ref), (depth_hbm.at[gcol], depth_ref),
                (ev_hbm, ev_ref), (ec_hbm, ec_ref), (occ_hbm, occ_ref),
            ]
        )
    ]
    for load in loads:
        load.start()
    loads[0].wait()

    freq = gmap_ref[...]
    freq = jnp.where(freq > LENGTH // 2, freq - LENGTH, freq)
    kx, ky, kz = freq[0:1], freq[1:2], freq[2:3]
    flip = kx < 0
    index_ref[0:1, :] = jnp.where(flip, -kx, kx) * SIDE + jnp.where(flip, -ky, ky) + REACH
    index_ref[1:2, :] = jnp.where(flip, -1, 1)
    index_ref[2:3, :] = kz + (REACH + HALF)
    pad = (CHUNKS - 1) * PLANES
    high_ref[pad:, 576:] = jnp.zeros((PLANES, CHUNK - 576), BF16)
    low_ref[pad:, 576:] = jnp.zeros((PLANES, CHUNK - 576), BF16)
    loads[1].wait()
    loads[2].wait()

    for chunk in range(CHUNKS):
        for begin, width in ((0, 384), (384, 384), (768, 384)) if chunk < 4 else ((0, 384), (384, 192)):
            span = pl.ds(chunk * CHUNK + begin, width)
            sub = lax.broadcasted_iota(jnp.int32, (8, width), 0)
            real, imag = [], []
            for d in range(DEPTH):
                v, w = [], []
                for c in range(2):
                    four = val_ref[c, d, :, span].astype(F32)
                    v.append(jnp.concatenate([four, four], axis=0))
                    two = cond_ref[c, d, :, span].astype(F32)
                    spread = [jnp.broadcast_to(two[i : i + 1], (8, width)) for i in range(2)]
                    w.append(jnp.where(sub < 4, spread[0], spread[1]))
                real.append(v[0] * w[0] + v[1] * w[1])
                imag.append(v[0] * w[1] - v[1] * w[0])
            field = jnp.concatenate(real + imag, axis=0)
            high = field.astype(BF16)
            low = (field - high.astype(F32)).astype(BF16)
            rows = slice(chunk * PLANES, (chunk + 1) * PLANES)
            high_ref[rows, begin : begin + width] = high
            low_ref[rows, begin : begin + width] = low

    for load in loads[3:]:
        load.wait()
    planes = dot(high_ref[...], table_ref[0]) + dot(low_ref[...], table_ref[0]) + dot(high_ref[...], table_ref[1])
    cos_sum = planes[0:PLANES, 0:256]
    sin_sum = planes[0:PLANES, 256:512]
    for chunk in range(1, CHUNKS):
        at = chunk * PLANES
        c_part, s_part = planes[at : at + PLANES, 0:256], planes[at : at + PLANES, 256:512]
        c_turn, s_turn = turn_ref[2 * chunk : 2 * chunk + 1, :], turn_ref[2 * chunk + 1 : 2 * chunk + 2, :]
        cos_sum += c_turn * c_part - s_turn * s_part
        sin_sum += s_turn * c_part + c_turn * s_part

    even = cos_sum
    odd = jnp.concatenate([sin_sum[72:144], -sin_sum[0:72]], axis=0)
    even_high, odd_high = even.astype(BF16), odd.astype(BF16)
    left_ref[0:144, :] = even_high
    left_ref[144:288, :] = (even - even_high.astype(F32)).astype(BF16)
    left_ref[288:352, :] = depth_ref[...]
    right_ref[0:144, :] = odd_high
    right_ref[144:288, :] = (odd - odd_high.astype(F32)).astype(BF16)

    place = lax.broadcasted_iota(jnp.int32, (256, 256), 0).astype(F32).astype(BF16)
    one, nil = jnp.ones((256, 256), BF16), jnp.zeros((256, 256), BF16)

    def block(step):
        target = (x + 3 - step) % 4
        for piece in range(5):
            span = pl.ds(pl.multiple_of(target * 1280 + piece * 256, 256), 256)
            hit = place == index_ref[0:1, span].astype(F32).astype(BF16)
            phase = place == index_ref[2:3, span].astype(F32).astype(BF16)
            pick = jnp.where(hit | phase, one, nil)
            signed = jnp.where(hit, jnp.broadcast_to(index_ref[1:2, span].astype(F32).astype(BF16), (256, 256)), nil)
            first = dot(left_ref[...], pick)
            second = dot(right_ref[...], signed)
            values = first[0:144] + first[144:288] + second[0:144] + second[144:288]
            phases = first[288:306] + first[320:338]
            real, imag = None, None
            for d in range(DEPTH):
                re, im = values[8 * d : 8 * d + 8], values[72 + 8 * d : 80 + 8 * d]
                c, s = phases[d : d + 1], phases[DEPTH + d : DEPTH + d + 1]
                r_term, i_term = re * c + im * s, im * c - re * s
                real = r_term if real is None else real + r_term
                imag = i_term if imag is None else imag + i_term
            both = jnp.concatenate([real, imag], axis=0)
            for q in range(2):
                at = piece * 256 + q * 128
                part[step, at // WIDTH, :, at % WIDTH : at % WIDTH + 128] = both[:, q * 128 : (q + 1) * 128]

    sib_copies = [
        remote(part.at[j, 1 - core], sib.at[j], sib_s.at[j], sib_r.at[j], device(x, y, z, 1 - core)) for j in range(4)
    ]
    x_copies = [remote(xout.at[j], xin.at[j], xs.at[j], xr.at[j], x_peer(3 - j)) for j in range(3)]
    for j in range(4):
        block(j)
        if j == 0:
            pl.semaphore_wait(barrier, len(peers) + 8 - is_source.astype(jnp.int32))
        sib_copies[j].start()
        if j > 0:
            sib_copies[j - 1].wait_recv()
            xout[j - 1] = part[j - 1, core] + sib[j - 1]
            x_copies[j - 1].start()

    pair = lax.broadcasted_iota(jnp.int32, (16, 1), 0) % 8
    e_val = jnp.zeros((16, 1), F32)
    e_cond = jnp.zeros((16, 1), F32)
    occupied = jnp.zeros((16, 1), F32)
    for b in range(4):
        e_val = jnp.where(pair % 4 == b, ev_ref[b], e_val)
        occupied = jnp.where(pair % 4 == b, occ_ref[b].astype(F32), occupied)
    for d in range(2):
        e_cond = jnp.where(pair // 4 == d, ec_ref[d], e_cond)
    factor = jnp.sqrt(occupied / (e_cond - e_val) * (1.0 / math.sqrt(512.0)))

    sib_copies[3].wait_recv()
    total = part[3, core] + sib[3]
    for j in range(3):
        x_copies[j].wait_recv()
        total += xin[j]
    scaled = total * factor
    gathered[z_hi, 0, 0] = scaled.astype(BF16)

    main, rest = pl.ds(0, MAIN), pl.ds(MAIN, WIDTH - MAIN)
    far_copies = [
        remote(gathered.at[z_hi, 0, 0], gathered.at[z_hi, 0, 0], fs.at[a], fr.at[z_hi], z_peer(4 * a)) for a in (2, 1, 3)
    ]

    def near_steps(q):
        return ((1, 1), (15, 3), (2 - 4 * ((q + 1) // 2 % 2), 2))

    def near_main(q):
        own = gathered.at[q, 0, 0, :, main]
        return [
            remote(own, gathered.at[q, 0, m, :, main], zs.at[q, m], zr.at[q, m], z_peer(step))
            for step, m in near_steps(q)
        ]

    def y_main(q):
        own = gathered.at[q, 0, :, :, main]
        return [remote(own, gathered.at[q, j, :, :, main], ys.at[q, j], yr.at[q, j], y_peer(j)) for j in (2, 1, 3)]

    def y_rest(q):
        own = gathered.at[q, 0, 0, :, rest]
        return [remote(own, gathered.at[q, j, 0, :, rest], vs.at[q, j], vr.at[q, j], y_peer(j)) for j in (2, 1, 3)]

    def near_rest(q):
        own = gathered.at[q, :, 0, :, rest]
        return [
            remote(own, gathered.at[q, :, m, :, rest], us.at[q, m], ur.at[q, m], z_peer(step))
            for step, m in near_steps(q)
        ]

    def start(copies):
        for copy in copies:
            copy.start()

    def arrived(copies):
        for copy in copies:
            copy.wait_recv()

    def pass_on(q):
        @pl.when(z_hi != q)
        def _():
            remote(gathered.at[q, 0, 0], gathered.at[q, 0, 0], fs.at[0], fr.at[q], z_peer(4)).wait_recv()
            start(near_main(q) + y_rest(q))

    def share_main(q):
        arrived(near_main(q))
        start(y_main(q))

    def share_rest(q):
        arrived(y_rest(q))
        start(near_rest(q))

    start(far_copies + near_main(z_hi) + y_rest(z_hi))

    def row_piece(b):
        y_to, z_to = 2 * core + b // 4, b % 4 * 4 + x
        slot = row_in.at[z_hi, (y_to - y + 4) % 4, (z_to - z + 16) % 4]
        far = remote(row_out.at[b], slot, ps.at[b], pr.at[z_hi], device(x, y_to, z_to, core))
        near = pltpu.make_async_copy(row_out.at[b], slot, pr.at[z_hi])
        return far, near, (y_to == y) & (z_to == z)

    for b in range(8):
        cut = scaled[:, b * ROWS : (b + 1) * ROWS]
        row_out[b] = jnp.concatenate([cut, jnp.zeros((16, 128 - ROWS), F32)], axis=1).astype(BF16)
        far, near, own = row_piece(b)
        pl.when(own)(near.start)
        pl.when(jnp.logical_not(own))(far.start)

    chosen = jnp.where(
        lax.broadcasted_iota(jnp.int32, (ROWS, 128), 1) == lax.broadcasted_iota(jnp.int32, (ROWS, 128), 0), 1.0, 0.0
    ).astype(BF16)
    k_row = lax.broadcasted_iota(jnp.int32, (256, 256), 0)
    k_col = lax.broadcasted_iota(jnp.int32, (256, 256), 1)
    is_real = k_col // 8 % 2 == 0
    turn_i = jnp.where(
        is_real & (k_row == k_col + 8), 1.0, jnp.where(~is_real & (k_row == k_col - 8), -1.0, 0.0)
    ).astype(BF16)

    def row_copy(j, step):
        return remote(row_buf.at[j], row_buf.at[j], rs.at[j, step], rr.at[j], g_peer(step))

    def share_rows(j):
        @pl.when(is_source)
        def _():
            pltpu.make_async_copy(row_in.at[j], row_in.at[j], pr.at[j]).wait()
            pieces = row_in[j].reshape(256, 128)
            rows = lax.dot_general(chosen, pieces, (((1,), (1,)), ((), ())), preferred_element_type=F32)
            row_buf[j] = rows.astype(BF16)
            for step in range(1, 8):
                row_copy(j, step).start()

    def use(j, first):
        arrived(y_main(j) + near_rest(j))

        @pl.when(jnp.logical_not(is_source))
        def _():
            row_copy(j, 1).wait_recv()

        rows = row_buf[j]
        rows_i = dot(rows, turn_i).astype(BF16)
        columns = gathered[j].reshape(256, WIDTH)
        real, imag = dot(rows, columns), dot(rows_i, columns)
        if first:
            out_ref[0] = real
            out_ref[1] = imag
        else:
            out_ref[0] += real
            out_ref[1] += imag

    pass_on(0)
    pass_on(1)
    pass_on(3)
    pass_on(2)
    share_main(0)
    share_rest(0)
    share_main(1)
    share_rest(1)
    share_rows(0)
    share_main(3)
    share_rest(3)
    share_rows(1)
    share_main(2)
    share_rest(2)
    share_rows(3)
    share_rows(2)
    use(0, True)
    use(1, False)
    use(3, False)
    use(2, False)

    for b in range(8):
        far, _, own = row_piece(b)
        pl.when(jnp.logical_not(own))(far.wait_send)

    @pl.when(is_source)
    def _():
        for j in range(4):
            for step in range(1, 8):
                row_copy(j, step).wait_send()

    for copy in sib_copies + x_copies + far_copies:
        copy.wait_send()
    for q in range(4):
        for copy in near_main(q) + y_main(q) + y_rest(q) + near_rest(q):
            copy.wait_send()


def shards(psi_val, psi_cond, energy_val, energy_cond, occupancy, gmap):
    table, turned = plane_tables()
    vmem = pl.BlockSpec(memory_space=pltpu.VMEM)
    hbm = pl.BlockSpec(memory_space=pltpu.HBM)
    dma = pltpu.SemaphoreType.DMA
    return pl.pallas_call(
        kernel,
        out_shape=jax.ShapeDtypeStruct((2, ROWS, WIDTH), F32),
        in_specs=[hbm] * 9,
        out_specs=vmem,
        scratch_shapes=[
            pltpu.VMEM((2, DEPTH, 4, 5184), BF16),
            pltpu.VMEM((2, DEPTH, 2, 5184), BF16),
            pltpu.VMEM((3, NG), jnp.int32),
            pltpu.SMEM((4,), F32),
            pltpu.SMEM((2,), F32),
            pltpu.SMEM((4,), jnp.int32),
            pltpu.VMEM((2, CHUNK, 512), BF16),
            pltpu.VMEM((16, 256), F32),
            pltpu.VMEM((64, 256), BF16),
            pltpu.VMEM((8, NG), jnp.int32),
            pltpu.VMEM((CHUNKS * PLANES, CHUNK), BF16),
            pltpu.VMEM((CHUNKS * PLANES, CHUNK), BF16),
            pltpu.VMEM((352, 256), BF16),
            pltpu.VMEM((288, 256), BF16),
            pltpu.VMEM((4, 2, 16, WIDTH), F32),
            pltpu.VMEM((4, 16, WIDTH), F32),
            pltpu.VMEM((3, 16, WIDTH), F32),
            pltpu.VMEM((3, 16, WIDTH), F32),
            pltpu.VMEM((4, 4, 4, 16, WIDTH), BF16),
            pltpu.VMEM((4, ROWS, 256), BF16),
            pltpu.VMEM((8, 16, 128), BF16),
            pltpu.VMEM((4, 4, 4, 16, 128), BF16),
            dma((9,)), dma((4,)), dma((4,)), dma((3,)), dma((3,)),
            dma((4,)), dma((4,)), dma((4, 4)), dma((4, 4)), dma((4, 4)), dma((4, 4)), dma((4, 8)), dma((4,)), dma((8,)), dma((4,)),
            dma((4, 4)), dma((4, 4)), dma((4, 4)), dma((4, 4)),
        ],
        compiler_params=pltpu.CompilerParams(
            collective_id=0, has_side_effects=True, vmem_limit_bytes=64 * 1024 * 1024
        ),
        cost_estimate=pl.CostEstimate(flops=8_000_000_000, bytes_accessed=6_000_000, transcendentals=0),
    )(
        jnp.swapaxes(psi_val, 1, 2), jnp.swapaxes(psi_cond, 1, 2), gmap, energy_val, energy_cond, occupancy,
        jnp.asarray(table), jnp.asarray(turned), jnp.asarray(depth_tables()),
    )


def solution(mesh):
    return jax.shard_map(
        shards,
        mesh=mesh,
        in_specs=(
            P(None, "val", "gcol", None),
            P(None, "cond", "gcol", None),
            P("val"),
            P("cond"),
            P("val"),
            P(),
        ),
        out_specs=P(None, ("val", "cond"), "gcol"),
        check_vma=False,
    )
```

```python
import math

import jax
import jax.numpy as jnp
import numpy as np
from jax import lax
from jax.experimental import pallas as pl
from jax.experimental.pallas import tpu as pltpu
from jax.sharding import PartitionSpec as P

MESH = pl.DeviceIdType.MESH
LENGTH = 72
NG = 5120
REACH = 10
SIDE = 2 * REACH + 1
HALF = (REACH + 1) * SIDE
CHUNK_X = 16
CHUNK = CHUNK_X * LENGTH
CHUNKS = 5
DEPTH = 9
WIDTH = 640
ROWS = 80
MAIN = 384
PLANES = 144
F32 = jnp.float32
BF16 = jnp.bfloat16


def split_bf16(table):
    high = table.astype(np.float32).astype(jnp.bfloat16)
    low = (table - high.astype(np.float64)).astype(np.float32).astype(jnp.bfloat16)
    return high, low


def plane_tables():
    point = np.arange(CHUNK)
    column = np.arange(HALF)
    kx, ky = column // SIDE, column % SIDE - REACH
    turns = (point[:, None] // LENGTH * kx[None] + point[:, None] % LENGTH * ky[None]) % LENGTH
    angles = turns * (2.0 * math.pi / LENGTH)
    table = np.zeros((CHUNK, 512))
    table[:, :HALF] = np.cos(angles) / LENGTH
    table[:, 256 : 256 + HALF] = np.sin(angles) / LENGTH
    high, low = split_bf16(table)
    turned = np.zeros((16, 256), np.float32)
    for chunk in range(CHUNKS):
        shift = (kx * CHUNK_X * chunk) % LENGTH * (2.0 * math.pi / LENGTH)
        turned[2 * chunk, :HALF] = np.cos(shift)
        turned[2 * chunk + 1, :HALF] = np.sin(shift)
    return np.stack([high, low]), turned


def depth_tables():
    kz = np.arange(SIDE) - REACH
    out = np.zeros((8, 64, 256), jnp.bfloat16)
    for group in range(8):
        z = group * DEPTH + np.arange(DEPTH)
        angles = (z[:, None] * kz[None]) % LENGTH * (2.0 * math.pi / LENGTH)
        rows = np.concatenate([np.cos(angles), np.sin(angles)]) / math.sqrt(LENGTH)
        high, low = split_bf16(rows)
        out[group, 0:18, HALF : HALF + SIDE] = high
        out[group, 32:50, HALF : HALF + SIDE] = low
    return out


def dot(a, b):
    return lax.dot_general(a, b, (((1,), (0,)), ((), ())), preferred_element_type=F32)


def kernel(
    val_hbm, cond_hbm, gmap_hbm, ev_hbm, ec_hbm, occ_hbm, table_hbm, turn_hbm, depth_hbm,
    out_ref,
    val_ref, cond_ref, gmap_ref, ev_ref, ec_ref, occ_ref, table_ref, turn_ref, depth_ref, index_ref, high_ref, low_ref, left_ref, right_ref,
    part, sib, xout, xin, gathered, row_buf, row_out, row_in,
    in_sem, sib_s, sib_r, xs, xr, fs, fr, zs, zr, ys, yr, rs, rr, ps, pr, vs, vr, us, ur,
):
    z_lo = lax.axis_index("val")
    cond = lax.axis_index("cond")
    gcol = lax.axis_index("gcol")
    y, z_hi = cond // 4, cond % 4
    z = z_hi * 4 + z_lo
    x, core = gcol // 2, gcol % 2

    def device(x_at, y_at, z_at, core_at):
        return (z_at % 4, y_at * 4 + z_at // 4, x_at * 2 + core_at)

    def z_peer(step):
        return device(x, y, (z + step + 16) % 16, core)

    def y_peer(step):
        return device(x, (y + step) % 4, z, core)

    def x_peer(step):
        return device((x + step) % 4, y, z, core)

    def g_peer(step):
        return (z_lo, cond, (gcol + step) % 8)

    def remote(src, dst, send, recv, target):
        return pltpu.make_async_remote_copy(
            src_ref=src, dst_ref=dst, send_sem=send, recv_sem=recv, device_id=target, device_id_type=MESH
        )

    peers = [g_peer(s) for s in range(1, 8)]
    peers += [z_peer(s) for s in (1, 2, 4, 8, 12, 14, 15)]
    peers += [y_peer(s) for s in (1, 2, 3)]
    loads = [
        pltpu.make_async_copy(src, dst, in_sem.at[n])
        for n, (src, dst) in enumerate(
            [
                (gmap_hbm, gmap_ref), (val_hbm, val_ref), (cond_hbm, cond_ref), (table_hbm.at[0], table_ref.at[0]), (table_hbm.at[1], table_ref.at[1]),
                (turn_hbm, turn_ref), (depth_hbm.at[gcol], depth_ref),
                (ev_hbm, ev_ref), (ec_hbm, ec_ref), (occ_hbm, occ_ref),
            ]
        )
    ]
    for load in loads:
        load.start()
    barrier = pltpu.get_barrier_semaphore()
    for peer in peers:
        pl.semaphore_signal(barrier, inc=1, device_id=peer, device_id_type=MESH)
    is_source = gcol == z_lo * 2 + cond // 8

    @pl.when(is_source)
    def _():
        for n in range(64):

            @pl.when(n != y * 16 + z)
            def _(n=n):
                pl.semaphore_signal(
                    barrier, inc=1, device_id=device(x, n // 16, n % 16, core), device_id_type=MESH
                )

    loads[0].wait()

    freq = gmap_ref[...]
    freq = jnp.where(freq > LENGTH // 2, freq - LENGTH, freq)
    kx, ky, kz = freq[0:1], freq[1:2], freq[2:3]
    flip = kx < 0
    index_ref[0:1, :] = jnp.where(flip, -kx, kx) * SIDE + jnp.where(flip, -ky, ky) + REACH
    index_ref[1:2, :] = jnp.where(flip, -1, 1)
    index_ref[2:3, :] = kz + (REACH + HALF)
    pad = (CHUNKS - 1) * PLANES
    high_ref[pad:, 576:] = jnp.zeros((PLANES, CHUNK - 576), BF16)
    low_ref[pad:, 576:] = jnp.zeros((PLANES, CHUNK - 576), BF16)
    loads[1].wait()
    loads[2].wait()

    for chunk in range(CHUNKS):
        for begin, width in ((0, 384), (384, 384), (768, 384)) if chunk < 4 else ((0, 384), (384, 192)):
            span = pl.ds(chunk * CHUNK + begin, width)
            sub = lax.broadcasted_iota(jnp.int32, (8, width), 0)
            real, imag = [], []
            for d in range(DEPTH):
                v, w = [], []
                for c in range(2):
                    four = val_ref[c, d, :, span].astype(F32)
                    v.append(jnp.concatenate([four, four], axis=0))
                    two = cond_ref[c, d, :, span].astype(F32)
                    spread = [jnp.broadcast_to(two[i : i + 1], (8, width)) for i in range(2)]
                    w.append(jnp.where(sub < 4, spread[0], spread[1]))
                real.append(v[0] * w[0] + v[1] * w[1])
                imag.append(v[0] * w[1] - v[1] * w[0])
            field = jnp.concatenate(real + imag, axis=0)
            high = field.astype(BF16)
            low = (field - high.astype(F32)).astype(BF16)
            rows = slice(chunk * PLANES, (chunk + 1) * PLANES)
            high_ref[rows, begin : begin + width] = high
            low_ref[rows, begin : begin + width] = low

    loads[3].wait()
    full = (CHUNKS - 1) * PLANES

    def transform(rows, depth):
        return dot(high_ref[rows, 0:depth], table_ref[0, 0:depth]) + dot(low_ref[rows, 0:depth], table_ref[0, 0:depth])

    def correction(rows, depth):
        return dot(high_ref[rows, 0:depth], table_ref[1, 0:depth])

    whole, half = slice(0, full), slice(full, full + PLANES)
    planes = transform(whole, CHUNK)
    tail = transform(half, 640)
    for load in loads[4:]:
        load.wait()
    planes += correction(whole, CHUNK)
    tail += correction(half, 640)
    cos_sum = planes[0:PLANES, 0:256]
    sin_sum = planes[0:PLANES, 256:512]
    for chunk in range(1, CHUNKS):
        at = chunk * PLANES
        held = planes[at : at + PLANES] if chunk < CHUNKS - 1 else tail
        c_part, s_part = held[:, 0:256], held[:, 256:512]
        c_turn, s_turn = turn_ref[2 * chunk : 2 * chunk + 1, :], turn_ref[2 * chunk + 1 : 2 * chunk + 2, :]
        cos_sum += c_turn * c_part - s_turn * s_part
        sin_sum += s_turn * c_part + c_turn * s_part

    even = cos_sum
    odd = jnp.concatenate([sin_sum[72:144], -sin_sum[0:72]], axis=0)
    even_high, odd_high = even.astype(BF16), odd.astype(BF16)
    left_ref[0:144, :] = even_high
    left_ref[144:288, :] = (even - even_high.astype(F32)).astype(BF16)
    left_ref[288:352, :] = depth_ref[...]
    right_ref[0:144, :] = odd_high
    right_ref[144:288, :] = (odd - odd_high.astype(F32)).astype(BF16)

    place = lax.broadcasted_iota(jnp.int32, (256, 256), 0).astype(F32).astype(BF16)
    one, nil = jnp.ones((256, 256), BF16), jnp.zeros((256, 256), BF16)

    def block(step):
        target = (x + 3 - step) % 4
        for piece in range(5):
            span = pl.ds(pl.multiple_of(target * 1280 + piece * 256, 256), 256)
            hit = place == index_ref[0:1, span].astype(F32).astype(BF16)
            phase = place == index_ref[2:3, span].astype(F32).astype(BF16)
            pick = jnp.where(hit | phase, one, nil)
            signed = jnp.where(hit, jnp.broadcast_to(index_ref[1:2, span].astype(F32).astype(BF16), (256, 256)), nil)
            first = dot(left_ref[...], pick)
            second = dot(right_ref[...], signed)
            values = first[0:144] + first[144:288] + second[0:144] + second[144:288]
            phases = first[288:306] + first[320:338]
            real, imag = None, None
            for d in range(DEPTH):
                re, im = values[8 * d : 8 * d + 8], values[72 + 8 * d : 80 + 8 * d]
                c, s = phases[d : d + 1], phases[DEPTH + d : DEPTH + d + 1]
                r_term, i_term = re * c + im * s, im * c - re * s
                real = r_term if real is None else real + r_term
                imag = i_term if imag is None else imag + i_term
            both = jnp.concatenate([real, imag], axis=0)
            for q in range(2):
                at = piece * 256 + q * 128
                part[step, at // WIDTH, :, at % WIDTH : at % WIDTH + 128] = both[:, q * 128 : (q + 1) * 128]

    sib_copies = [
        remote(part.at[j, 1 - core], sib.at[j], sib_s.at[j], sib_r.at[j], device(x, y, z, 1 - core)) for j in range(4)
    ]
    x_copies = [remote(xout.at[j], xin.at[j], xs.at[j], xr.at[j], x_peer(3 - j)) for j in range(3)]
    for j in range(4):
        block(j)
        if j == 0:
            pl.semaphore_wait(barrier, len(peers) + 8 - is_source.astype(jnp.int32))
        sib_copies[j].start()
        if j > 0:
            sib_copies[j - 1].wait_recv()
            xout[j - 1] = part[j - 1, core] + sib[j - 1]
            x_copies[j - 1].start()

    pair = lax.broadcasted_iota(jnp.int32, (16, 1), 0) % 8
    e_val = jnp.zeros((16, 1), F32)
    e_cond = jnp.zeros((16, 1), F32)
    occupied = jnp.zeros((16, 1), F32)
    for b in range(4):
        e_val = jnp.where(pair % 4 == b, ev_ref[b], e_val)
        occupied = jnp.where(pair % 4 == b, occ_ref[b].astype(F32), occupied)
    for d in range(2):
        e_cond = jnp.where(pair // 4 == d, ec_ref[d], e_cond)
    factor = jnp.sqrt(occupied / (e_cond - e_val) * (1.0 / math.sqrt(512.0)))

    sib_copies[3].wait_recv()
    total = part[3, core] + sib[3]
    for j in range(3):
        x_copies[j].wait_recv()
        total += xin[j]
    scaled = total * factor
    gathered[z_hi, 0, 0] = scaled.astype(BF16)

    main, rest = pl.ds(0, MAIN), pl.ds(MAIN, WIDTH - MAIN)
    far_copies = [
        remote(gathered.at[z_hi, 0, 0], gathered.at[z_hi, 0, 0], fs.at[a], fr.at[z_hi], z_peer(4 * a)) for a in (2, 1, 3)
    ]

    def near_steps(q):
        return ((1, 1), (15, 3), (2 - 4 * ((q + 1) // 2 % 2), 2))

    def near_main(q):
        own = gathered.at[q, 0, 0, :, main]
        return [
            remote(own, gathered.at[q, 0, m, :, main], zs.at[q, m], zr.at[q, m], z_peer(step))
            for step, m in near_steps(q)
        ]

    def y_main(g):
        own = gathered.at[pl.ds(2 * g, 2), 0, :, :, main]
        return [
            remote(own, gathered.at[pl.ds(2 * g, 2), j, :, :, main], ys.at[g, j], yr.at[g, j], y_peer(j))
            for j in (2, 1, 3)
        ]

    def y_rest(q):
        own = gathered.at[q, 0, 0, :, rest]
        return [remote(own, gathered.at[q, j, 0, :, rest], vs.at[q, j], vr.at[q, j], y_peer(j)) for j in (2, 1, 3)]

    def near_rest(g):
        own = gathered.at[pl.ds(2 * g, 2), :, 0, :, rest]
        return [
            remote(own, gathered.at[pl.ds(2 * g, 2), :, m, :, rest], us.at[g, m], ur.at[g, m], z_peer(step))
            for step, m in near_steps(g)
        ]

    def start(copies):
        for copy in copies:
            copy.start()

    def arrived(copies):
        for copy in copies:
            copy.wait_recv()

    def pass_on(q):
        @pl.when(z_hi != q)
        def _():
            remote(gathered.at[q, 0, 0], gathered.at[q, 0, 0], fs.at[0], fr.at[q], z_peer(4)).wait_recv()
            start(near_main(q) + y_rest(q))

    def share_main(g):
        arrived(near_main(2 * g) + near_main(2 * g + 1))
        start(y_main(g))

    def share_rest(g):
        arrived(y_rest(2 * g) + y_rest(2 * g + 1))
        start(near_rest(g))

    start(far_copies + near_main(z_hi) + y_rest(z_hi))

    def row_piece(b):
        y_to, z_to = 2 * core + b // 4, b % 4 * 4 + x
        slot = row_in.at[z_hi, (y_to - y + 4) % 4, (z_to - z + 16) % 4]
        far = remote(row_out.at[b], slot, ps.at[b], pr.at[z_hi], device(x, y_to, z_to, core))
        near = pltpu.make_async_copy(row_out.at[b], slot, pr.at[z_hi])
        return far, near, (y_to == y) & (z_to == z)

    for b in range(8):
        cut = scaled[:, b * ROWS : (b + 1) * ROWS]
        row_out[b] = jnp.concatenate([cut, jnp.zeros((16, 128 - ROWS), F32)], axis=1).astype(BF16)
        far, near, own = row_piece(b)
        pl.when(own)(near.start)
        pl.when(jnp.logical_not(own))(far.start)

    chosen = jnp.where(
        lax.broadcasted_iota(jnp.int32, (ROWS, 128), 1) == lax.broadcasted_iota(jnp.int32, (ROWS, 128), 0), 1.0, 0.0
    ).astype(BF16)
    k_row = lax.broadcasted_iota(jnp.int32, (256, 256), 0)
    k_col = lax.broadcasted_iota(jnp.int32, (256, 256), 1)
    is_real = k_col // 8 % 2 == 0
    turn_i = jnp.where(
        is_real & (k_row == k_col + 8), 1.0, jnp.where(~is_real & (k_row == k_col - 8), -1.0, 0.0)
    ).astype(BF16)

    def row_copy(g, step):
        held = row_buf.at[pl.ds(2 * g, 2)]
        return remote(held, held, rs.at[g, step], rr.at[g], g_peer(step))

    def share_rows(g):
        @pl.when(is_source)
        def _():
            for j in (2 * g, 2 * g + 1):
                pltpu.make_async_copy(row_in.at[j], row_in.at[j], pr.at[j]).wait()
                pieces = row_in[j].reshape(256, 128)
                rows = lax.dot_general(chosen, pieces, (((1,), (1,)), ((), ())), preferred_element_type=F32)
                row_buf[j] = rows.astype(BF16)
            for step in range(1, 8):
                row_copy(g, step).start()

    def ready(g):
        arrived(y_main(g) + near_rest(g))

        @pl.when(jnp.logical_not(is_source))
        def _():
            row_copy(g, 1).wait_recv()

    def use(j, first):
        rows = row_buf[j]
        rows_i = dot(rows, turn_i).astype(BF16)
        columns = gathered[j].reshape(256, WIDTH)
        real, imag = dot(rows, columns), dot(rows_i, columns)
        if first:
            out_ref[0] = real
            out_ref[1] = imag
        else:
            out_ref[0] += real
            out_ref[1] += imag

    pass_on(0)
    pass_on(1)
    pass_on(3)
    pass_on(2)
    share_rows(0)
    share_main(0)
    share_rest(0)
    share_rows(1)
    share_main(1)
    share_rest(1)
    ready(0)
    use(0, True)
    use(1, False)
    ready(1)
    use(3, False)
    use(2, False)

    for b in range(8):
        far, _, own = row_piece(b)
        pl.when(jnp.logical_not(own))(far.wait_send)

    @pl.when(is_source)
    def _():
        for g in range(2):
            for step in range(1, 8):
                row_copy(g, step).wait_send()

    for copy in sib_copies + x_copies + far_copies:
        copy.wait_send()
    for q in range(4):
        for copy in near_main(q) + y_rest(q):
            copy.wait_send()
    for g in range(2):
        for copy in y_main(g) + near_rest(g):
            copy.wait_send()


def shards(psi_val, psi_cond, energy_val, energy_cond, occupancy, gmap):
    table, turned = plane_tables()
    vmem = pl.BlockSpec(memory_space=pltpu.VMEM)
    hbm = pl.BlockSpec(memory_space=pltpu.HBM)
    dma = pltpu.SemaphoreType.DMA
    return pl.pallas_call(
        kernel,
        out_shape=jax.ShapeDtypeStruct((2, ROWS, WIDTH), F32),
        in_specs=[hbm] * 9,
        out_specs=vmem,
        scratch_shapes=[
            pltpu.VMEM((2, DEPTH, 4, 5184), BF16),
            pltpu.VMEM((2, DEPTH, 2, 5184), BF16),
            pltpu.VMEM((3, NG), jnp.int32),
            pltpu.SMEM((4,), F32),
            pltpu.SMEM((2,), F32),
            pltpu.SMEM((4,), jnp.int32),
            pltpu.VMEM((2, CHUNK, 512), BF16),
            pltpu.VMEM((16, 256), F32),
            pltpu.VMEM((64, 256), BF16),
            pltpu.VMEM((8, NG), jnp.int32),
            pltpu.VMEM((CHUNKS * PLANES, CHUNK), BF16),
            pltpu.VMEM((CHUNKS * PLANES, CHUNK), BF16),
            pltpu.VMEM((352, 256), BF16),
            pltpu.VMEM((288, 256), BF16),
            pltpu.VMEM((4, 2, 16, WIDTH), F32),
            pltpu.VMEM((4, 16, WIDTH), F32),
            pltpu.VMEM((3, 16, WIDTH), F32),
            pltpu.VMEM((3, 16, WIDTH), F32),
            pltpu.VMEM((4, 4, 4, 16, WIDTH), BF16),
            pltpu.VMEM((4, ROWS, 256), BF16),
            pltpu.VMEM((8, 16, 128), BF16),
            pltpu.VMEM((4, 4, 4, 16, 128), BF16),
            dma((10,)), dma((4,)), dma((4,)), dma((3,)), dma((3,)),
            dma((4,)), dma((4,)), dma((4, 4)), dma((4, 4)), dma((4, 4)), dma((4, 4)), dma((4, 8)), dma((4,)), dma((8,)), dma((4,)),
            dma((4, 4)), dma((4, 4)), dma((4, 4)), dma((4, 4)),
        ],
        compiler_params=pltpu.CompilerParams(
            collective_id=0, has_side_effects=True, vmem_limit_bytes=64 * 1024 * 1024
        ),
        cost_estimate=pl.CostEstimate(flops=8_000_000_000, bytes_accessed=6_000_000, transcendentals=0),
    )(
        jnp.swapaxes(psi_val, 1, 2), jnp.swapaxes(psi_cond, 1, 2), gmap, energy_val, energy_cond, occupancy,
        jnp.asarray(table), jnp.asarray(turned), jnp.asarray(depth_tables()),
    )


def solution(mesh):
    return jax.shard_map(
        shards,
        mesh=mesh,
        in_specs=(
            P(None, "val", "gcol", None),
            P(None, "cond", "gcol", None),
            P("val"),
            P("cond"),
            P("val"),
            P(),
        ),
        out_specs=P(None, ("val", "cond"), "gcol"),
        check_vma=False,
    )
```

```python
import math

import jax
import jax.numpy as jnp
import numpy as np
from jax import lax
from jax.experimental import pallas as pl
from jax.experimental.pallas import tpu as pltpu
from jax.sharding import PartitionSpec as P

MESH = pl.DeviceIdType.MESH
LENGTH = 72
NG = 5120
REACH = 10
SIDE = 2 * REACH + 1
HALF = (REACH + 1) * SIDE
CHUNK_X = 16
CHUNK = CHUNK_X * LENGTH
CHUNKS = 5
DEPTH = 9
WIDTH = 640
ROWS = 80
MAIN = 384
PLANES = 144
F32 = jnp.float32
BF16 = jnp.bfloat16


def split_bf16(table):
    high = table.astype(np.float32).astype(jnp.bfloat16)
    low = (table - high.astype(np.float64)).astype(np.float32).astype(jnp.bfloat16)
    return high, low


def plane_tables():
    point = np.arange(CHUNK)
    column = np.arange(HALF)
    kx, ky = column // SIDE, column % SIDE - REACH
    turns = (point[:, None] // LENGTH * kx[None] + point[:, None] % LENGTH * ky[None]) % LENGTH
    angles = turns * (2.0 * math.pi / LENGTH)
    table = np.zeros((CHUNK, 512))
    table[:, :HALF] = np.cos(angles) / LENGTH
    table[:, 256 : 256 + HALF] = np.sin(angles) / LENGTH
    high, low = split_bf16(table)
    turned = np.zeros((16, 256), np.float32)
    for chunk in range(CHUNKS):
        shift = (kx * CHUNK_X * chunk) % LENGTH * (2.0 * math.pi / LENGTH)
        turned[2 * chunk, :HALF] = np.cos(shift)
        turned[2 * chunk + 1, :HALF] = np.sin(shift)
    return np.stack([high, low]), turned


def depth_tables():
    kz = np.arange(SIDE) - REACH
    out = np.zeros((8, 64, 256), jnp.bfloat16)
    for group in range(8):
        z = group * DEPTH + np.arange(DEPTH)
        angles = (z[:, None] * kz[None]) % LENGTH * (2.0 * math.pi / LENGTH)
        rows = np.concatenate([np.cos(angles), np.sin(angles)]) / math.sqrt(LENGTH)
        high, low = split_bf16(rows)
        out[group, 0:18, HALF : HALF + SIDE] = high
        out[group, 32:50, HALF : HALF + SIDE] = low
    return out


def dot(a, b):
    return lax.dot_general(a, b, (((1,), (0,)), ((), ())), preferred_element_type=F32)


def kernel(
    val_hbm, cond_hbm, gmap_hbm, ev_hbm, ec_hbm, occ_hbm, table_hbm, turn_hbm, depth_hbm,
    out_ref,
    val_ref, cond_ref, gmap_ref, ev_ref, ec_ref, occ_ref, table_ref, turn_ref, depth_ref, index_ref, high_ref, low_ref, left_ref, right_ref,
    part, sib, xout, xin, gathered, row_buf, row_out, row_in,
    in_sem, sib_s, sib_r, xs, xr, fs, fr, zs, zr, ys, yr, rs, rr, ps, pr, vs, vr, us, ur,
):
    z_lo = lax.axis_index("val")
    cond = lax.axis_index("cond")
    gcol = lax.axis_index("gcol")
    y, z_hi = cond // 4, cond % 4
    z = z_hi * 4 + z_lo
    x, core = gcol // 2, gcol % 2

    def device(x_at, y_at, z_at, core_at):
        return (z_at % 4, y_at * 4 + z_at // 4, x_at * 2 + core_at)

    def z_peer(step):
        return device(x, y, (z + step + 16) % 16, core)

    def y_peer(step):
        return device(x, (y + step) % 4, z, core)

    def x_peer(step):
        return device((x + step) % 4, y, z, core)

    def g_peer(step):
        return (z_lo, cond, (gcol + step) % 8)

    def remote(src, dst, send, recv, target):
        return pltpu.make_async_remote_copy(
            src_ref=src, dst_ref=dst, send_sem=send, recv_sem=recv, device_id=target, device_id_type=MESH
        )

    peers = [g_peer(s) for s in range(1, 8)]
    peers += [z_peer(s) for s in (1, 2, 4, 8, 12, 14, 15)]
    peers += [y_peer(s) for s in (1, 2, 3)]
    loads = [
        pltpu.make_async_copy(src, dst, in_sem.at[n])
        for n, (src, dst) in enumerate(
            [
                (gmap_hbm, gmap_ref), (val_hbm, val_ref), (cond_hbm, cond_ref), (table_hbm.at[0], table_ref.at[0]), (table_hbm.at[1], table_ref.at[1]),
                (turn_hbm, turn_ref), (depth_hbm.at[gcol], depth_ref),
                (ev_hbm, ev_ref), (ec_hbm, ec_ref), (occ_hbm, occ_ref),
            ]
        )
    ]
    for load in loads:
        load.start()
    barrier = pltpu.get_barrier_semaphore()
    for peer in peers:
        pl.semaphore_signal(barrier, inc=1, device_id=peer, device_id_type=MESH)
    is_source = gcol == z_lo * 2 + cond // 8

    @pl.when(is_source)
    def _():
        for n in range(64):

            @pl.when(n != y * 16 + z)
            def _(n=n):
                pl.semaphore_signal(
                    barrier, inc=1, device_id=device(x, n // 16, n % 16, core), device_id_type=MESH
                )

    loads[0].wait()

    freq = gmap_ref[...]
    freq = jnp.where(freq > LENGTH // 2, freq - LENGTH, freq)
    kx, ky, kz = freq[0:1], freq[1:2], freq[2:3]
    flip = kx < 0
    index_ref[0:1, :] = jnp.where(flip, -kx, kx) * SIDE + jnp.where(flip, -ky, ky) + REACH
    index_ref[1:2, :] = jnp.where(flip, -1, 1)
    index_ref[2:3, :] = kz + (REACH + HALF)
    pad = (CHUNKS - 1) * PLANES
    high_ref[pad:, 576:] = jnp.zeros((PLANES, CHUNK - 576), BF16)
    low_ref[pad:, 576:] = jnp.zeros((PLANES, CHUNK - 576), BF16)
    loads[1].wait()
    loads[2].wait()

    for chunk in range(CHUNKS):
        for begin, width in ((0, 384), (384, 384), (768, 384)) if chunk < 4 else ((0, 384), (384, 192)):
            span = pl.ds(chunk * CHUNK + begin, width)
            sub = lax.broadcasted_iota(jnp.int32, (8, width), 0)
            real, imag = [], []
            for d in range(DEPTH):
                v, w = [], []
                for c in range(2):
                    four = val_ref[c, d, :, span].astype(F32)
                    v.append(jnp.concatenate([four, four], axis=0))
                    two = cond_ref[c, d, :, span].astype(F32)
                    spread = [jnp.broadcast_to(two[i : i + 1], (8, width)) for i in range(2)]
                    w.append(jnp.where(sub < 4, spread[0], spread[1]))
                real.append(v[0] * w[0] + v[1] * w[1])
                imag.append(v[0] * w[1] - v[1] * w[0])
            field = jnp.concatenate(real + imag, axis=0)
            high = field.astype(BF16)
            low = (field - high.astype(F32)).astype(BF16)
            rows = slice(chunk * PLANES, (chunk + 1) * PLANES)
            high_ref[rows, begin : begin + width] = high
            low_ref[rows, begin : begin + width] = low

    loads[3].wait()
    full = (CHUNKS - 1) * PLANES

    def transform(rows, depth):
        return dot(high_ref[rows, 0:depth], table_ref[0, 0:depth]) + dot(low_ref[rows, 0:depth], table_ref[0, 0:depth])

    def correction(rows, depth):
        return dot(high_ref[rows, 0:depth], table_ref[1, 0:depth])

    whole, half = slice(0, full), slice(full, full + PLANES)
    planes = transform(whole, CHUNK)
    tail = transform(half, 640)
    for load in loads[4:]:
        load.wait()
    planes += correction(whole, CHUNK)
    tail += correction(half, 640)
    cos_sum = planes[0:PLANES, 0:256]
    sin_sum = planes[0:PLANES, 256:512]
    for chunk in range(1, CHUNKS):
        at = chunk * PLANES
        held = planes[at : at + PLANES] if chunk < CHUNKS - 1 else tail
        c_part, s_part = held[:, 0:256], held[:, 256:512]
        c_turn, s_turn = turn_ref[2 * chunk : 2 * chunk + 1, :], turn_ref[2 * chunk + 1 : 2 * chunk + 2, :]
        cos_sum += c_turn * c_part - s_turn * s_part
        sin_sum += s_turn * c_part + c_turn * s_part

    even = cos_sum
    odd = jnp.concatenate([sin_sum[72:144], -sin_sum[0:72]], axis=0)
    even_high, odd_high = even.astype(BF16), odd.astype(BF16)
    left_ref[0:144, :] = even_high
    left_ref[144:288, :] = (even - even_high.astype(F32)).astype(BF16)
    left_ref[288:352, :] = depth_ref[...]
    right_ref[0:144, :] = odd_high
    right_ref[144:288, :] = (odd - odd_high.astype(F32)).astype(BF16)

    place = lax.broadcasted_iota(jnp.int32, (256, 256), 0).astype(F32).astype(BF16)
    one, nil = jnp.ones((256, 256), BF16), jnp.zeros((256, 256), BF16)

    def block(step):
        target = (x + 3 - step) % 4
        for piece in range(5):
            span = pl.ds(pl.multiple_of(target * 1280 + piece * 256, 256), 256)
            hit = place == index_ref[0:1, span].astype(F32).astype(BF16)
            phase = place == index_ref[2:3, span].astype(F32).astype(BF16)
            pick = jnp.where(hit | phase, one, nil)
            signed = jnp.where(hit, jnp.broadcast_to(index_ref[1:2, span].astype(F32).astype(BF16), (256, 256)), nil)
            first = dot(left_ref[...], pick)
            second = dot(right_ref[...], signed)
            values = first[0:144] + first[144:288] + second[0:144] + second[144:288]
            phases = first[288:306] + first[320:338]
            real, imag = None, None
            for d in range(DEPTH):
                re, im = values[8 * d : 8 * d + 8], values[72 + 8 * d : 80 + 8 * d]
                c, s = phases[d : d + 1], phases[DEPTH + d : DEPTH + d + 1]
                r_term, i_term = re * c + im * s, im * c - re * s
                real = r_term if real is None else real + r_term
                imag = i_term if imag is None else imag + i_term
            both = jnp.concatenate([real, imag], axis=0)
            for q in range(2):
                at = piece * 256 + q * 128
                part[step, at // WIDTH, :, at % WIDTH : at % WIDTH + 128] = both[:, q * 128 : (q + 1) * 128]

    sib_copies = [
        remote(part.at[j, 1 - core], sib.at[j], sib_s.at[j], sib_r.at[j], device(x, y, z, 1 - core)) for j in range(4)
    ]
    x_copies = [remote(xout.at[j], xin.at[j], xs.at[j], xr.at[j], x_peer(3 - j)) for j in range(3)]
    for j in range(4):
        block(j)
        if j == 0:
            pl.semaphore_wait(barrier, len(peers) + 8 - is_source.astype(jnp.int32))
        sib_copies[j].start()
        if j > 0:
            sib_copies[j - 1].wait_recv()
            xout[j - 1] = part[j - 1, core] + sib[j - 1]
            x_copies[j - 1].start()

    pair = lax.broadcasted_iota(jnp.int32, (16, 1), 0) % 8
    e_val = jnp.zeros((16, 1), F32)
    e_cond = jnp.zeros((16, 1), F32)
    occupied = jnp.zeros((16, 1), F32)
    for b in range(4):
        e_val = jnp.where(pair % 4 == b, ev_ref[b], e_val)
        occupied = jnp.where(pair % 4 == b, occ_ref[b].astype(F32), occupied)
    for d in range(2):
        e_cond = jnp.where(pair // 4 == d, ec_ref[d], e_cond)
    factor = jnp.sqrt(occupied / (e_cond - e_val) * (1.0 / math.sqrt(512.0)))

    sib_copies[3].wait_recv()
    total = part[3, core] + sib[3]
    for j in range(3):
        x_copies[j].wait_recv()
        total += xin[j]
    scaled = total * factor
    gathered[z_hi, 0, 0] = scaled.astype(BF16)

    main, rest = pl.ds(0, MAIN), pl.ds(MAIN, WIDTH - MAIN)
    far_copies = [
        remote(gathered.at[z_hi, 0, 0], gathered.at[z_hi, 0, 0], fs.at[a], fr.at[z_hi], z_peer(4 * a)) for a in (2, 1, 3)
    ]

    def near_steps(q):
        return ((1, 1), (15, 3), (2 - 4 * ((q + 1) // 2 % 2), 2))

    def near_main(q):
        own = gathered.at[q, 0, 0, :, main]
        return [
            remote(own, gathered.at[q, 0, m, :, main], zs.at[q, m], zr.at[q, m], z_peer(step))
            for step, m in near_steps(q)
        ]

    def y_main(g):
        own = gathered.at[pl.ds(2 * g, 2), 0, :, :, main]
        return [
            remote(own, gathered.at[pl.ds(2 * g, 2), j, :, :, main], ys.at[g, j], yr.at[g, j], y_peer(j))
            for j in (2, 1, 3)
        ]

    def y_rest(q):
        own = gathered.at[q, 0, 0, :, rest]
        return [remote(own, gathered.at[q, j, 0, :, rest], vs.at[q, j], vr.at[q, j], y_peer(j)) for j in (2, 1, 3)]

    def near_rest(g):
        own = gathered.at[pl.ds(2 * g, 2), :, 0, :, rest]
        return [
            remote(own, gathered.at[pl.ds(2 * g, 2), :, m, :, rest], us.at[g, m], ur.at[g, m], z_peer(step))
            for step, m in near_steps(g)
        ]

    def start(copies):
        for copy in copies:
            copy.start()

    def arrived(copies):
        for copy in copies:
            copy.wait_recv()

    def pass_on(q):
        @pl.when(z_hi != q)
        def _():
            remote(gathered.at[q, 0, 0], gathered.at[q, 0, 0], fs.at[0], fr.at[q], z_peer(4)).wait_recv()
            start(near_main(q) + y_rest(q))

    def share_main(g):
        arrived(near_main(2 * g) + near_main(2 * g + 1))
        start(y_main(g))

    def share_rest(g):
        arrived(y_rest(2 * g) + y_rest(2 * g + 1))
        start(near_rest(g))

    start(far_copies + near_main(z_hi) + y_rest(z_hi))

    def row_piece(b):
        y_to, z_to = 2 * core + b // 4, b % 4 * 4 + x
        slot = row_in.at[z_hi, (y_to - y + 4) % 4, (z_to - z + 16) % 4]
        far = remote(row_out.at[b], slot, ps.at[b], pr.at[z_hi], device(x, y_to, z_to, core))
        near = pltpu.make_async_copy(row_out.at[b], slot, pr.at[z_hi])
        return far, near, (y_to == y) & (z_to == z)

    for b in range(8):
        cut = scaled[:, b * ROWS : (b + 1) * ROWS]
        row_out[b] = jnp.concatenate([cut, jnp.zeros((16, 128 - ROWS), F32)], axis=1).astype(BF16)
        far, near, own = row_piece(b)
        pl.when(own)(near.start)
        pl.when(jnp.logical_not(own))(far.start)

    chosen = jnp.where(
        lax.broadcasted_iota(jnp.int32, (ROWS, 128), 1) == lax.broadcasted_iota(jnp.int32, (ROWS, 128), 0), 1.0, 0.0
    ).astype(BF16)
    k_row = lax.broadcasted_iota(jnp.int32, (256, 256), 0)
    k_col = lax.broadcasted_iota(jnp.int32, (256, 256), 1)
    is_real = k_col // 8 % 2 == 0
    turn_i = jnp.where(
        is_real & (k_row == k_col + 8), 1.0, jnp.where(~is_real & (k_row == k_col - 8), -1.0, 0.0)
    ).astype(BF16)

    def row_copy(g, step):
        held = row_buf.at[pl.ds(2 * g, 2)]
        return remote(held, held, rs.at[g, step], rr.at[g], g_peer(step))

    def share_rows(g):
        @pl.when(is_source)
        def _():
            for j in (2 * g, 2 * g + 1):
                pltpu.make_async_copy(row_in.at[j], row_in.at[j], pr.at[j]).wait()
                pieces = row_in[j].reshape(256, 128)
                rows = lax.dot_general(chosen, pieces, (((1,), (1,)), ((), ())), preferred_element_type=F32)
                row_buf[j] = rows.astype(BF16)
            for step in range(1, 8):
                row_copy(g, step).start()

    def ready(g):
        arrived(y_main(g) + near_rest(g))

        @pl.when(jnp.logical_not(is_source))
        def _():
            row_copy(g, 1).wait_recv()

    def use(g, first):
        rows = [row_buf[2 * g], row_buf[2 * g + 1]]
        rows_i = jnp.concatenate([dot(r, turn_i).astype(BF16) for r in rows], axis=1)
        rows = jnp.concatenate(rows, axis=1)
        columns = gathered[2 * g : 2 * g + 2].reshape(512, WIDTH)
        real, imag = dot(rows, columns), dot(rows_i, columns)
        if first:
            out_ref[0] = real
            out_ref[1] = imag
        else:
            out_ref[0] += real
            out_ref[1] += imag

    pass_on(0)
    pass_on(1)
    pass_on(3)
    pass_on(2)
    share_rows(0)
    share_main(0)
    share_rest(0)
    share_rows(1)
    share_main(1)
    share_rest(1)
    ready(0)
    use(0, True)
    ready(1)
    use(1, False)

    for b in range(8):
        far, _, own = row_piece(b)
        pl.when(jnp.logical_not(own))(far.wait_send)

    @pl.when(is_source)
    def _():
        for g in range(2):
            for step in range(1, 8):
                row_copy(g, step).wait_send()

    for copy in sib_copies + x_copies + far_copies:
        copy.wait_send()
    for q in range(4):
        for copy in near_main(q) + y_rest(q):
            copy.wait_send()
    for g in range(2):
        for copy in y_main(g) + near_rest(g):
            copy.wait_send()


def shards(psi_val, psi_cond, energy_val, energy_cond, occupancy, gmap):
    table, turned = plane_tables()
    vmem = pl.BlockSpec(memory_space=pltpu.VMEM)
    hbm = pl.BlockSpec(memory_space=pltpu.HBM)
    dma = pltpu.SemaphoreType.DMA
    return pl.pallas_call(
        kernel,
        out_shape=jax.ShapeDtypeStruct((2, ROWS, WIDTH), F32),
        in_specs=[hbm] * 9,
        out_specs=vmem,
        scratch_shapes=[
            pltpu.VMEM((2, DEPTH, 4, 5184), BF16),
            pltpu.VMEM((2, DEPTH, 2, 5184), BF16),
            pltpu.VMEM((3, NG), jnp.int32),
            pltpu.SMEM((4,), F32),
            pltpu.SMEM((2,), F32),
            pltpu.SMEM((4,), jnp.int32),
            pltpu.VMEM((2, CHUNK, 512), BF16),
            pltpu.VMEM((16, 256), F32),
            pltpu.VMEM((64, 256), BF16),
            pltpu.VMEM((8, NG), jnp.int32),
            pltpu.VMEM((CHUNKS * PLANES, CHUNK), BF16),
            pltpu.VMEM((CHUNKS * PLANES, CHUNK), BF16),
            pltpu.VMEM((352, 256), BF16),
            pltpu.VMEM((288, 256), BF16),
            pltpu.VMEM((4, 2, 16, WIDTH), F32),
            pltpu.VMEM((4, 16, WIDTH), F32),
            pltpu.VMEM((3, 16, WIDTH), F32),
            pltpu.VMEM((3, 16, WIDTH), F32),
            pltpu.VMEM((4, 4, 4, 16, WIDTH), BF16),
            pltpu.VMEM((4, ROWS, 256), BF16),
            pltpu.VMEM((8, 16, 128), BF16),
            pltpu.VMEM((4, 4, 4, 16, 128), BF16),
            dma((10,)), dma((4,)), dma((4,)), dma((3,)), dma((3,)),
            dma((4,)), dma((4,)), dma((4, 4)), dma((4, 4)), dma((4, 4)), dma((4, 4)), dma((4, 8)), dma((4,)), dma((8,)), dma((4,)),
            dma((4, 4)), dma((4, 4)), dma((4, 4)), dma((4, 4)),
        ],
        compiler_params=pltpu.CompilerParams(
            collective_id=0, has_side_effects=True, vmem_limit_bytes=64 * 1024 * 1024
        ),
        cost_estimate=pl.CostEstimate(flops=8_000_000_000, bytes_accessed=6_000_000, transcendentals=0),
    )(
        jnp.swapaxes(psi_val, 1, 2), jnp.swapaxes(psi_cond, 1, 2), gmap, energy_val, energy_cond, occupancy,
        jnp.asarray(table), jnp.asarray(turned), jnp.asarray(depth_tables()),
    )


def solution(mesh):
    return jax.shard_map(
        shards,
        mesh=mesh,
        in_specs=(
            P(None, "val", "gcol", None),
            P(None, "cond", "gcol", None),
            P("val"),
            P("cond"),
            P("val"),
            P(),
        ),
        out_specs=P(None, ("val", "cond"), "gcol"),
        check_vma=False,
    )
```
